256 devices in a mesh: graph: 128 (over y, x, z), mp: 2 (over core).
Axes of the slice: x: 4, y: 4, z: 8, core: 2. Of those that a mesh axis runs over, the one named last changes fastest.
Arguments:
- nodes_in: bfloat16 [262144, 512], P('graph'), may hold values from -24 to 24
- query: bfloat16 [262144, 512], P('graph', 'mp'), may hold values from -200 to 200
- keys: bfloat16 [262144, 512], P('graph', 'mp'), may hold values from -6.5 to 6.5
- values: bfloat16 [262144, 512], P('graph', 'mp'), may hold values from -6 to 6
- grad_attn: bfloat16 [262144, 512], P('graph', 'mp'), may hold values from -6 to 6
- w_query: bfloat16 [512, 512], P(None, 'mp'), may hold values from -0.25 to 0.25
- w_key: bfloat16 [512, 512], P(None, 'mp'), may hold values from -0.25 to 0.25
- w_value: bfloat16 [512, 512], P(None, 'mp'), may hold values from -0.25 to 0.25
- halo_owner: int32 [32768, 1], P('graph'), may hold values from 0 to 127; in each aligned block of 256 rows (0 to 255, 256 to 511, ...) at most 4 rows name the same one
- halo_row: int32 [32768], P('graph'), may hold values from 0 to 2047
- pattern: int32 [2048, 2], P('graph'), may hold values 0 or 1
Outputs:
- grad_nodes: bfloat16 [262144, 512], P('graph', 'mp')
- grad_weights: float32 [512, 3, 512], P('graph', None, 'mp')
The draws below stay inside these ranges and needn't reach their ends.
Inputs may be any that keep to these rules, and one draw needn't show every extreme that they name: `halo_owner`: among the 256 reads of one partition no owner appears more than 4 times, and some owner appears exactly 4 times.
All inputs are finite; a program needn't handle non-finite values. No bound on the sum of `pattern` on one device may be relied on, other than what follows from the above.
Results may differ from the reference program's by a relative error of at most 0.014.
Values may be sent and summed in bfloat16 or wider, within the bound.
A program may use at most 128 MiB of HBM per device.

```python
import math
import jax
import jax.numpy as jnp
import numpy as np
from jax import lax

D = 512
HEADS = 8
BLK = 128
ROWS_DEV = 2048
HR = 256
NODES = 262144
BLOCKS = 2048
HB = 2
HALO_ALL = 32768
CAP = 4
N_GRAPH = 128


def shared_keys(key):
    return jnp.clip(jax.random.normal(key, (NODES, D), jnp.float32), -6.0, 6.0)


def draw_keys(key, part):
    base = shared_keys(key)
    return base.astype(jnp.bfloat16)


def draw_query(key, part):
    key = jax.random.fold_in(key, 13)
    fresh = jnp.clip(jax.random.normal(key, (NODES, D), jnp.float32), -6.0, 6.0)
    return fresh.astype(jnp.bfloat16)


def with_ends(result, rng, least, high):
    index_at = [jax.random.randint(jax.random.fold_in(rng, axis), (), 0, length) for axis, length in enumerate(result.shape)]
    main_axis = result.shape.index(max(result.shape))
    next_to = index_at[:main_axis] + [(index_at[main_axis] + 1) % result.shape[main_axis]] + index_at[main_axis + 1:]
    return result.at[tuple(index_at)].set(least).at[tuple(next_to)].set(high)


def spiked(drawn, stream_key, source, target, shards_of, factor):
    owner, partner = [(jnp.arange(drawn.shape[dim]) // (drawn.shape[dim] // shards_of)).reshape([-1 if axis == dim else 1 for axis in range(drawn.ndim)]) for dim in (source, target)]
    chosen = jax.random.permutation(stream_key, shards_of)[partner]
    strong = (owner == chosen) | (owner == (partner + shards_of // 2) % shards_of)
    return jnp.where(strong, factor * drawn, drawn)


def steps_of(own_key, shape, split, low, top_value):
    gain = 1.0
    for dim, shards_of in split:
        heights = jax.random.uniform(jax.random.fold_in(jax.random.fold_in(own_key, 6), dim), (shards_of,), jnp.float32, low / len(split), top_value / len(split))
        gain = gain * jnp.repeat(jnp.exp(heights), shape[dim] // shards_of).reshape((-1,) + (1,) * (len(shape) - 1 - dim))
    return gain


def assign_block(own_key, own, number, rows, number_of, top, reach, lean):
    sequence = jax.random.permutation(own_key, number_of)
    heavy_load, usual = load_shares(number_of, rows * top, reach, lean, True), load_shares(number_of, rows * top, reach, lean, False)
    places = jnp.arange(number_of)

    def named(tallies, turn):
        used = int((tallies > 0).sum())
        fixed = max(1, used // 4)
        shifted = fixed + (places - fixed + turn * (used - fixed)) % max(1, number_of - fixed)
        return jnp.zeros((number_of,), jnp.int32).at[sequence[jnp.where(places < fixed, places, shifted)]].set(jnp.asarray(tallies, jnp.int32))

    tallies = jnp.where(number % 4 == 0, named(heavy_load, number // 4), named(usual, number - number // 4 - 1))
    mixed = jax.random.permutation(jax.random.fold_in(own, 3), number_of)
    giver, receiver = mixed[0:number_of // 2 * 2:2], mixed[1:number_of // 2 * 2:2]
    room = jnp.minimum(tallies[giver] - 1, reach - tallies[receiver]) // 2
    room = jnp.where((giver == sequence[0]) | (receiver == sequence[0]) | (tallies[receiver] == 0), 0, jnp.maximum(room, 0))
    shifted = jax.random.randint(jax.random.fold_in(own, 4), (number_of // 2,), 0, 1 << 20) % (room + 1)
    tallies = tallies.at[giver].add(-shifted).at[receiver].add(shifted)
    items = jnp.searchsorted(jnp.cumsum(tallies), jnp.arange(rows * top), side="right").astype(jnp.int32)
    listing = items.reshape(top, rows).T
    listing = listing[jax.random.permutation(jax.random.fold_in(own, 1), rows)]
    turn = jax.random.randint(jax.random.fold_in(own, 2), (rows, 1), 0, top)
    return jnp.take_along_axis(listing, (jnp.arange(top)[None, :] + turn) % top, axis=1)


def load_shares(amount, total, reach, lean, full):
    loads = [(1 << 20) // math.isqrt(standing ** lean) + 1 for standing in range(1, amount + 1)]
    largest = reach if full else min(reach, max(-(-total // amount), total * loads[0] // sum(loads)))
    least = 1 if total - largest >= amount - 1 else 0
    counts, spare = [largest] + [least] * (amount - 1), total - largest - least * (amount - 1)
    while spare > 0:
        candidates = [i for i in range(1, amount) if counts[i] < largest] or [i for i in range(1, amount) if counts[i] < reach]
        whole, left = sum([loads[i] for i in candidates]), spare
        for i in candidates:
            addition = min(reach - counts[i], max(1, left * loads[i] // whole), spare)
            counts[i] = counts[i] + addition
            spare = spare - addition
    return np.array(counts)


def bell_draw(key, dims, deviation, most, pieces=(), dtype=jnp.bfloat16):
    result = deviation * jax.random.normal(key, dims, jnp.float32)
    if pieces:
        result = result * steps_of(key, dims, pieces, -0.22, 0.18)
    return jnp.clip(result, -most, most).astype(dtype)


def bell_draw_with(own_key, dims, width, bound, split, heavy, kind=jnp.bfloat16):
    drawn = width * jax.random.normal(own_key, dims, jnp.float32)
    if split:
        drawn = drawn * steps_of(own_key, dims, split, -0.22, 0.18)
    return jnp.clip(spiked(drawn, jax.random.fold_in(own_key, 3), *heavy), -bound, bound).astype(kind)


def setup_inputs(seed: int = 0) -> dict:
    seeds = jax.random.split(jax.random.key(seed), 12)
    nodes_in = bell_draw_with(seeds[0], (NODES, D), 1.0, 24.0, ((0, 128),), (0, 1, 128, 5.5))
    query = draw_query(jax.random.fold_in(seeds[11], 71), 0)
    keys = draw_keys(jax.random.fold_in(seeds[11], 71), 0)
    values = bell_draw(seeds[3], (NODES, D), 1.0, 6.0, ((0, 128), (1, 2)))
    grad_attn = bell_draw(seeds[4], (NODES, D), 1.0, 6.0, ((0, 128), (1, 2)))
    w_query = bell_draw(seeds[5], (D, D), D ** -0.5, 0.25, ((1, 2),))
    w_key = bell_draw(seeds[6], (D, D), D ** -0.5, 0.25, ((1, 2),))
    w_value = bell_draw(seeds[7], (D, D), D ** -0.5, 0.25, ((1, 2),))
    halo_owner_keys = jax.random.split(jax.random.fold_in(seeds[8], 1), HALO_ALL // HR)
    halo_owner_turns = jax.random.permutation(jax.random.fold_in(seeds[8], 3), HALO_ALL // HR)
    halo_owner = jax.vmap(lambda own, number: assign_block(jax.random.fold_in(seeds[8], 2), own, number, HR, N_GRAPH, 1, CAP, 2))(halo_owner_keys, halo_owner_turns).reshape((HALO_ALL, 1))
    halo_row = with_ends(jax.random.randint(seeds[9], (HALO_ALL,), 0, ROWS_DEV), jax.random.fold_in(seeds[9], 1), 0, ROWS_DEV - 1).astype(jnp.int32)
    pattern = with_ends((jax.random.randint(seeds[10], (BLOCKS, HB), 0, 2) < 1).astype(jnp.int32), jax.random.fold_in(seeds[10], 1), 0, 1)
    return dict(nodes_in=nodes_in, query=query, keys=keys, values=values, grad_attn=grad_attn, w_query=w_query, w_key=w_key, w_value=w_value, halo_owner=halo_owner, halo_row=halo_row, pattern=pattern)


def rounded(value):
    return lax.optimization_barrier(value.astype(jnp.bfloat16)).astype(jnp.float32)

def attend_blocks(queries_b, keys_b, values_b, douts_b, halo_keys, halo_values, visible, scale):
    scores_own = jnp.einsum('bqhe,bkhe->bhqk', queries_b, keys_b) * scale
    scores_far = jnp.einsum('bqhe,khe->bhqk', queries_b, halo_keys) * scale
    scores_far = jnp.where(visible, scores_far, -1e+30)
    highest = jnp.maximum(lax.optimization_barrier(jnp.max(scores_own, -1, keepdims=True)), lax.optimization_barrier(jnp.max(scores_far, -1, keepdims=True)))
    weight_own = jnp.exp(scores_own - highest)
    weight_far = jnp.where(visible, jnp.exp(scores_far - highest), 0.0)
    totals = lax.optimization_barrier(jnp.sum(weight_own, -1, keepdims=True)) + lax.optimization_barrier(jnp.sum(weight_far, -1, keepdims=True))
    prob_own = weight_own / totals
    prob_far = weight_far / totals
    dprob_own = jnp.einsum('bqhe,bkhe->bhqk', douts_b, values_b)
    dprob_far = jnp.einsum('bqhe,khe->bhqk', douts_b, halo_values)
    row_term = lax.optimization_barrier(jnp.sum(prob_own * dprob_own, -1, keepdims=True)) + lax.optimization_barrier(jnp.sum(prob_far * dprob_far, -1, keepdims=True))
    slope_own = rounded(prob_own * (dprob_own - row_term))
    slope_far = rounded(prob_far * (dprob_far - row_term))
    low_own = rounded(prob_own)
    low_far = rounded(prob_far)
    grad_q = scale * (jnp.einsum('bhqk,bkhe->bqhe', slope_own, keys_b) + jnp.einsum('bhqk,khe->bqhe', slope_far, halo_keys))
    grad_k_own = scale * jnp.einsum('bhqk,bqhe->bkhe', slope_own, queries_b)
    grad_k_far = scale * jnp.einsum('bhqk,bqhe->khe', slope_far, queries_b)
    grad_v_own = jnp.einsum('bhqk,bqhe->bkhe', low_own, douts_b)
    grad_v_far = jnp.einsum('bhqk,bqhe->khe', low_far, douts_b)
    return (grad_q, grad_k_own, grad_v_own, grad_k_far, grad_v_far)

def reference(nodes_in, query, keys, values, grad_attn, w_query, w_key, w_value, halo_owner, halo_row, pattern):
    head_size = D // HEADS
    blocks_dev = ROWS_DEV // BLK
    scale = 1.0 / math.sqrt(head_size)
    halo_ids = (halo_owner[:, 0] * ROWS_DEV + halo_row).astype(jnp.int32)
    shape_blocks = (blocks_dev, BLK, HEADS, head_size)

    def partition(inputs):
        q_part, k_part, v_part, d_part, ids_part, mask_part = inputs
        halo_keys = keys[ids_part].astype(jnp.float32).reshape(HR, HEADS, head_size)
        halo_values = values[ids_part].astype(jnp.float32).reshape(HR, HEADS, head_size)
        visible = (jnp.repeat(mask_part, BLK, axis=1) > 0)[:, None, None, :]
        outputs = attend_blocks(q_part.astype(jnp.float32).reshape(shape_blocks), k_part.astype(jnp.float32).reshape(shape_blocks), v_part.astype(jnp.float32).reshape(shape_blocks), d_part.astype(jnp.float32).reshape(shape_blocks), halo_keys, halo_values, visible, scale)
        grad_q, grad_k_own, grad_v_own, grad_k_far, grad_v_far = outputs
        return (grad_q.reshape(ROWS_DEV, D), grad_k_own.reshape(ROWS_DEV, D), grad_v_own.reshape(ROWS_DEV, D), grad_k_far.reshape(HR, D), grad_v_far.reshape(HR, D))
    stacked_inputs = (query.reshape(N_GRAPH, ROWS_DEV, D), keys.reshape(N_GRAPH, ROWS_DEV, D), values.reshape(N_GRAPH, ROWS_DEV, D), grad_attn.reshape(N_GRAPH, ROWS_DEV, D), halo_ids.reshape(N_GRAPH, HR), pattern.reshape(N_GRAPH, blocks_dev, HB))
    grad_q, grad_k_own, grad_v_own, grad_k_far, grad_v_far = lax.map(partition, stacked_inputs)
    grad_k = grad_k_own.reshape(NODES, D).at[halo_ids].add(grad_k_far.reshape(HALO_ALL, D))
    grad_v = grad_v_own.reshape(NODES, D).at[halo_ids].add(grad_v_far.reshape(HALO_ALL, D))
    grad_query = grad_q.reshape(NODES, D).astype(jnp.bfloat16)
    grad_key = grad_k.astype(jnp.bfloat16)
    grad_value = grad_v.astype(jnp.bfloat16)
    summed = jnp.dot(grad_query, w_query.T, preferred_element_type=jnp.float32) + jnp.dot(grad_key, w_key.T, preferred_element_type=jnp.float32) + jnp.dot(grad_value, w_value.T, preferred_element_type=jnp.float32)
    grad_nodes = summed.astype(jnp.bfloat16)
    grad_weights = jnp.stack([jnp.dot(nodes_in.T, grad_query, preferred_element_type=jnp.float32), jnp.dot(nodes_in.T, grad_key, preferred_element_type=jnp.float32), jnp.dot(nodes_in.T, grad_value, preferred_element_type=jnp.float32)], axis=1)
    return (grad_nodes, grad_weights)
```

```python
import functools
import math

import jax
import jax.numpy as jnp
from jax import lax
from jax.experimental import pallas as pl
from jax.experimental.pallas import tpu as pltpu
from jax.sharding import PartitionSpec as P

MESH = pl.DeviceIdType.MESH
F32 = jnp.float32
BF16 = jnp.bfloat16
I32 = jnp.int32

HEADS_LOCAL = 4
E = 64
BLK = 128
ROWS = 2048
W = 256
HR = 256
CAP = 4
NX, NY, NZ = 4, 4, 8
NG = NX * NY * NZ
NPLANE = NX * NY
HALF = NG // 2
LOG2E = 1.4426950408889634
NT = (((1,), (1,)), ((), ()))
TN = (((0,), (0,)), ((), ()))


def dot(a, b, dims=(((1,), (0,)), ((), ()))):
    return lax.dot_general(a, b, dims, preferred_element_type=F32)


def iota(shape, dim):
    return lax.broadcasted_iota(I32, shape, dim)


def place():
    me = lax.axis_index("graph")
    mp = lax.axis_index("mp")
    return me, mp, lax.div(me, NZ), lax.rem(me, NZ)


def peer(plane, z, dplane, dz):
    return lax.rem(plane + dplane, NPLANE) * NZ + lax.rem(z + dz, NZ)


def peer_back(plane, z, k):
    dplane, dz = lax.div(k, NZ), lax.rem(k, NZ)
    return lax.rem(plane - dplane + NPLANE, NPLANE) * NZ + lax.rem(z - dz + NZ, NZ)


def relative(owner, plane, z):
    dplane = ((owner >> 3) - plane + NPLANE) & (NPLANE - 1)
    dz = ((owner & 7) - z + NZ) & (NZ - 1)
    return dplane, dz


def rank_column(owner_c, owner_r):
    same = (owner_c == owner_r) & (iota((HR, HR), 1) < iota((HR, HR), 0))
    return jnp.sum(jnp.where(same, 1, 0), axis=1, keepdims=True)


def rank_row(owner_c, owner_r):
    same = (owner_c == owner_r) & (iota((HR, HR), 0) < iota((HR, HR), 1))
    return jnp.sum(jnp.where(same, 1, 0), axis=0, keepdims=True)


def onehot(mask):
    return jnp.where(mask, 1.0, 0.0).astype(BF16)


def wait_bytes(ref, sem):
    pltpu.make_async_copy(ref, ref, sem).wait()


def send(src, dst, ssem, rsem, dev):
    pltpu.make_async_remote_copy(
        src_ref=src, dst_ref=dst, send_sem=ssem, recv_sem=rsem, device_id=dev, device_id_type=MESH
    ).start()


def greet_all(me, mp, plane, z):
    barrier = pltpu.get_barrier_semaphore()

    @pl.loop(1, NG)
    def _(k):
        p = peer(plane, z, lax.div(k, NZ), lax.rem(k, NZ))
        pl.semaphore_signal(barrier, inc=1, device_id=(p, mp), device_id_type=MESH)

    pl.semaphore_signal(barrier, inc=1, device_id=(me, 1 - mp), device_id_type=MESH)
    return barrier


def gather_kernel(
    owner_c_ref, owner_r_ref, row_r_ref, keys_hbm, values_hbm, nodes_hbm,
    halo_ref, far_nodes_ref, asked_ref,
    kbuf, vbuf, nbuf, s1, r1, s2, r2, fst, kv_send, kv_recv, n_send, n_recv, stack, other,
    lsem, ssem, rsem,
):
    me, mp, plane, z = place()
    loads = [
        pltpu.make_async_copy(keys_hbm, kbuf, lsem.at[0]),
        pltpu.make_async_copy(values_hbm, vbuf, lsem.at[1]),
        pltpu.make_async_copy(nodes_hbm, nbuf, lsem.at[2]),
    ]
    for load in loads:
        load.start()
    barrier = greet_all(me, mp, plane, z)

    owner_c, owner_r, row_r = owner_c_ref[...], owner_r_ref[...], row_r_ref[...]
    rank_c = rank_column(owner_c, owner_r)
    dplane_c, dz_c = relative(owner_c, plane, z)
    _, dz_r = relative(owner_r, plane, z)
    lane_c = dplane_c * CAP + rank_c
    column = onehot(lane_c == iota((HR, 128), 1))
    value = row_r + 1
    at_z = dz_r == iota((NZ, HR), 0)
    high = jnp.where(at_z, value >> 6, 0).astype(F32).astype(BF16)
    low = jnp.where(at_z, value & 63, 0).astype(F32).astype(BF16)
    wanted = (dot(high, column) * 64.0 + dot(low, column)).astype(I32) - 1
    for dz in range(NZ):
        s1[dz] = jnp.broadcast_to(wanted[dz : dz + 1, :], (8, 128))
    pl.semaphore_wait(barrier, NG)

    for dz in range(1, NZ):
        send(s1.at[dz], r1.at[dz], ssem.at[0], rsem.at[0], (peer(plane, z, 0, dz), mp))
    r1[0] = s1[0]
    wait_bytes(r1.at[pl.ds(0, NZ - 1)], rsem.at[0])
    sub = iota((8, 128), 0)
    gathered = jnp.zeros((8, 128), I32)
    for dz in range(NZ):
        gathered = jnp.where(sub == dz, r1[dz], gathered)
    s2[...] = gathered
    for dp in range(1, NPLANE):
        send(s2, r2.at[dp], ssem.at[1], rsem.at[1], (peer(plane, z, dp, 0), mp))
    r2[0] = gathered
    wait_bytes(r2.at[pl.ds(0, NPLANE - 1)], rsem.at[1])

    table = r2[...].reshape(NG, 128)
    table_t = table.T
    lanes, subs = iota((NG, 128), 1), iota((NG, 128), 0)
    asked = []
    for j in range(CAP):
        asked.append(
            jnp.sum(jnp.where(lanes == (subs >> 3) * CAP + j, table, 0), axis=1, keepdims=True)
        )
        asked_ref[j : j + 1, :] = jnp.sum(
            jnp.where(subs == (lanes >> 3) * CAP + j, table_t, 0), axis=0, keepdims=True
        )
    asked_ref[CAP:8, :] = jnp.zeros((8 - CAP, 128), I32)

    loads[0].wait()
    loads[1].wait()
    for j in range(CAP):
        pick = onehot(asked[j] == iota((NG, ROWS), 1))
        part_k = dot(pick, kbuf[...])
        part_v = dot(pick, vbuf[...])
        for c in range(2):
            fst[pl.ds(4 * j + c, NG, stride=16), :] = part_k[:, c * 128 : (c + 1) * 128]
            fst[pl.ds(4 * j + 2 + c, NG, stride=16), :] = part_v[:, c * 128 : (c + 1) * 128]
    kv_send[...] = fst[...].reshape(NG, 16, 128).astype(BF16)

    @pl.loop(1, NG)
    def _(k):
        p = peer_back(plane, z, k)
        send(kv_send.at[k], kv_recv.at[k], ssem.at[2], rsem.at[2], (p, mp))

    kv_recv[0] = kv_send[0]

    loads[2].wait()
    for j in range(CAP):
        pick = onehot(asked[j] == iota((NG, ROWS), 1))
        part_n = dot(pick, nbuf[...])
        for c in range(4):
            fst[pl.ds(4 * j + c, NG, stride=16), :] = part_n[:, c * 128 : (c + 1) * 128]
    n_send[...] = fst[...].reshape(NG, 16, 128).astype(BF16)

    @pl.loop(1, HALF)
    def _(i):
        k = mp * HALF + i
        p = peer_back(plane, z, k)
        send(n_send.at[k], n_recv.at[i], ssem.at[3], rsem.at[3], (p, mp))

    @pl.when(mp == 1)
    def _():
        p = peer_back(plane, z, HALF)
        send(n_send.at[HALF], n_recv.at[0], ssem.at[4], rsem.at[4], (p, mp))
        wait_bytes(n_recv.at[0], ssem.at[4])
        wait_bytes(n_recv.at[0], rsem.at[4])

    @pl.when(mp == 0)
    def _():
        n_recv[0] = n_send[0]

    wait_bytes(kv_recv.at[pl.ds(0, NG - 1)], rsem.at[2])
    fst[...] = kv_recv[...].astype(F32).reshape(NG * 16, 128)
    for j in range(CAP):
        for c in range(4):
            stack[j * NG : (j + 1) * NG, c * 128 : (c + 1) * 128] = fst[
                pl.ds(4 * j + c, NG, stride=16), :
            ].astype(BF16)
    k_c = dplane_c * NZ + dz_c
    place_mat = onehot(rank_c * NG + k_c == iota((HR, CAP * NG), 1))
    halo_ref[...] = dot(place_mat, stack[...]).astype(BF16)

    wait_bytes(n_recv.at[pl.ds(0, HALF - 1)], rsem.at[3])
    fst[0 : HALF * 16, :] = n_recv[...].astype(F32).reshape(HALF * 16, 128)
    for j in range(CAP):
        for c in range(4):
            stack[j * HALF : (j + 1) * HALF, c * 128 : (c + 1) * 128] = fst[
                pl.ds(4 * j + c, HALF, stride=16), :
            ].astype(BF16)
    k_h = k_c - mp * HALF
    slot = jnp.where((k_h >= 0) & (k_h < HALF), rank_c * HALF + k_h, -1)
    place_half = onehot(slot == iota((HR, CAP * HALF), 1))
    mine = dot(place_half, stack[0 : CAP * HALF, :]).astype(BF16)
    s3 = stack.at[pl.ds(CAP * HALF, HR)]
    s3[...] = mine
    send(s3, other, ssem.at[5], rsem.at[5], (me, 1 - mp))
    wait_bytes(other, rsem.at[5])
    far_nodes_ref[...] = mine + other[...]

    wait_bytes(s1.at[pl.ds(0, NZ - 1)], ssem.at[0])
    wait_bytes(r2.at[pl.ds(0, NPLANE - 1)], ssem.at[1])
    wait_bytes(kv_send.at[pl.ds(0, NG - 1)], ssem.at[2])
    wait_bytes(n_recv.at[pl.ds(0, HALF - 1)], ssem.at[3])
    wait_bytes(other, ssem.at[5])


def attention_kernel(
    pattern_ref, q_ref, k_ref, v_ref, g_ref, n_ref, halo_ref, far_nodes_ref, wq_ref, wk_ref, wv_ref,
    t_ref, gw_ref, mine_ref, other_ref,
    far_kt, far_acc,
):
    step = pl.program_id(0)
    mp = lax.axis_index("mp")
    far_k = halo_ref[:, 0:W]
    far_v = halo_ref[:, W : 2 * W]

    @pl.when(step == 0)
    def _():
        far_kt[...] = (far_k * 0.125).T
        far_acc[...] = jnp.zeros_like(far_acc)
        gw_ref[...] = jnp.zeros_like(gw_ref)

    head_of_lane = iota((BLK, W), 1) // E
    slopes_far, lows_far, queries, grads = [], [], [], []
    for sub in range(2):
        rows = slice(sub * BLK, (sub + 1) * BLK)
        q = q_ref[rows, :] * 0.125
        g = g_ref[rows, :]
        k = k_ref[rows, :]
        v = v_ref[rows, :]
        qm = jnp.concatenate(
            [jnp.where(head_of_lane == h, q, 0.0).astype(BF16) for h in range(HEADS_LOCAL)], 0
        )
        gm = jnp.concatenate(
            [jnp.where(head_of_lane == h, g, 0.0).astype(BF16) for h in range(HEADS_LOCAL)], 0
        )
        bias = [
            jnp.where(pattern_ref[2 * step + sub, h] > 0, 0.0, 1e30).astype(F32) for h in range(2)
        ]
        s_own = dot(k, qm, NT)
        s_far = dot(far_k, qm, NT)
        top = jnp.maximum(
            jnp.max(s_own, 0, keepdims=True),
            jnp.maximum(
                jnp.max(s_far[0:BLK], 0, keepdims=True) - bias[0],
                jnp.max(s_far[BLK:], 0, keepdims=True) - bias[1],
            ),
        )
        p_own = jnp.exp2((s_own - top) * LOG2E)
        p_far = jnp.concatenate(
            [
                jnp.exp2((s_far[0:BLK] - (top + bias[0])) * LOG2E),
                jnp.exp2((s_far[BLK:] - (top + bias[1])) * LOG2E),
            ],
            0,
        )
        total = jnp.sum(p_own, 0, keepdims=True) + jnp.sum(p_far, 0, keepdims=True)
        inv = 1.0 / total
        d_own = dot(v, gm, NT)
        d_far = dot(far_v, gm, NT)
        prob_own = p_own * inv
        prob_far = p_far * inv
        term = jnp.sum(prob_own * d_own, 0, keepdims=True) + jnp.sum(
            prob_far * d_far, 0, keepdims=True
        )
        slope_own = (prob_own * (d_own - term)).astype(BF16)
        slope_far = (prob_far * (d_far - term)).astype(BF16)
        low_own = prob_own.astype(BF16)
        low_far = prob_far.astype(BF16)
        dk = dot(slope_own, qm)
        dv = dot(low_own, gm)
        kt = (k * 0.125).T
        dqt = jnp.concatenate(
            [
                dot(kt[h * E : (h + 1) * E, :], slope_own[:, h * BLK : (h + 1) * BLK])
                + dot(far_kt[h * E : (h + 1) * E, :], slope_far[:, h * BLK : (h + 1) * BLK])
                for h in range(HEADS_LOCAL)
            ],
            0,
        )
        dq = dqt.T
        grads.append((dq.astype(BF16), dk.astype(BF16), dv.astype(BF16)))
        slopes_far.append(slope_far)
        lows_far.append(low_far)
        queries.append((qm, gm))

    slope2 = jnp.concatenate(slopes_far, 1)
    low2 = jnp.concatenate(lows_far, 1)
    qm2 = jnp.concatenate([a for a, _ in queries], 0)
    gm2 = jnp.concatenate([b for _, b in queries], 0)
    far_acc[:, 0:W] += dot(slope2, qm2)
    far_acc[:, W : 2 * W] += dot(low2, gm2)

    nodes = n_ref[...]
    mine = jnp.zeros((2 * BLK, W), F32)
    other = jnp.zeros((2 * BLK, W), F32)
    mine_rows = pl.ds(pl.multiple_of(mp * W, W), W)
    other_rows = pl.ds(pl.multiple_of((1 - mp) * W, W), W)
    for i, w_ref in enumerate((wq_ref, wk_ref, wv_ref)):
        grad = jnp.concatenate([grads[0][i], grads[1][i]], 0)
        gw_ref[:, i * W : (i + 1) * W] += dot(nodes, grad, TN)
        mine += dot(grad, w_ref[mine_rows, :], NT)
        other += dot(grad, w_ref[other_rows, :], NT)
    mine_ref[...] = mine
    other_ref[...] = other.astype(BF16)

    @pl.when(step == pl.num_programs(0) - 1)
    def _():
        dk_far = far_acc[:, 0:W].astype(BF16)
        dv_far = far_acc[:, W : 2 * W].astype(BF16)
        far_nodes = far_nodes_ref[...]
        t_ref[...] = (dot(dk_far, wk_ref[...], NT) + dot(dv_far, wv_ref[...], NT)).astype(BF16)
        gw_ref[:, W : 2 * W] += dot(far_nodes, dk_far, TN)
        gw_ref[:, 2 * W : 3 * W] += dot(far_nodes, dv_far, TN)


def return_kernel(
    owner_c_ref, owner_r_ref, asked_ref, t_ref, gw_hbm, mine_hbm, other_hbm,
    nodes_out, weights_out,
    gw, mine, e_recv, t_recv, fst, z_send, z_recv, x_send, z_full,
    y_send, y_recv, xx_send, xx_recv, zz_send, zz_recv,
    lsem, ssem, rsem,
):
    me, mp, plane, z = place()
    loads = [
        pltpu.make_async_copy(gw_hbm, gw, lsem.at[0]),
        pltpu.make_async_copy(mine_hbm, mine, lsem.at[1]),
    ]
    for load in loads:
        load.start()
    barrier = greet_all(me, mp, plane, z)
    owner_c, owner_r = owner_c_ref[...], owner_r_ref[...]
    rank_r = rank_row(owner_c, owner_r)
    dplane_r, dz_r = relative(owner_r, plane, z)
    k_h = dplane_r * NZ + dz_r - mp * HALF
    slot = jnp.where((k_h >= 0) & (k_h < HALF), rank_r * HALF + k_h, -1)
    place_t = onehot(slot == iota((CAP * HALF, HR), 0))
    pl.semaphore_wait(barrier, NG)

    twin = (me, 1 - mp)
    send(t_ref, t_recv, ssem.at[0], rsem.at[0], twin)
    send(other_hbm, e_recv, ssem.at[1], rsem.at[1], twin)
    loads[0].wait()
    y, x = lax.div(plane, NX), lax.rem(plane, NX)
    y_send[...] = gw[...].astype(BF16).reshape(NY, 128, 3 * W)
    for d in range(1, NY):
        yy = lax.rem(y + d, NY)
        send(y_send.at[yy], y_recv.at[d - 1], ssem.at[2], rsem.at[2], ((yy * NX + x) * NZ + z, mp))

    wait_bytes(t_recv, rsem.at[0])
    summed = (t_ref[...].astype(F32) + t_recv[...].astype(F32)).astype(BF16)
    placed = dot(place_t, summed)
    for j in range(CAP):
        for c in range(4):
            fst[pl.ds(4 * j + c, HALF, stride=16), :] = placed[
                j * HALF : (j + 1) * HALF, c * 128 : (c + 1) * 128
            ]
    z_send[...] = fst[...].reshape(HALF, 16, 128).astype(BF16)

    @pl.loop(1, HALF)
    def _(i):
        k = mp * HALF + i
        p = peer(plane, z, lax.div(k, NZ), lax.rem(k, NZ))
        send(z_send.at[i], z_recv.at[i], ssem.at[3], rsem.at[3], (p, mp))

    @pl.when(mp == 1)
    def _():
        p = peer(plane, z, HALF // NZ, 0)
        send(z_send.at[0], z_recv.at[0], ssem.at[4], rsem.at[4], (p, mp))
        wait_bytes(z_recv.at[0], ssem.at[4])
        wait_bytes(z_recv.at[0], rsem.at[4])

    @pl.when(mp == 0)
    def _():
        z_recv[0] = z_send[0]

    wait_bytes(y_recv, rsem.at[2])
    own = gw[pl.ds(pl.multiple_of(y * 128, 128), 128), :]
    for d in range(NY - 1):
        own += y_recv[d].astype(F32)
    gw[0:128, :] = own
    xx_send[...] = own.astype(BF16).reshape(NX, 32, 3 * W)
    for d in range(1, NX):
        xx = lax.rem(x + d, NX)
        send(xx_send.at[xx], xx_recv.at[d - 1], ssem.at[5], rsem.at[5], ((y * NX + xx) * NZ + z, mp))

    wait_bytes(z_recv.at[pl.ds(0, HALF - 1)], rsem.at[3])
    fst[...] = z_recv[...].astype(F32).reshape(HALF * 16, 128)
    for j in range(CAP):
        for c in range(2):
            x_send[j, :, c * 128 : (c + 1) * 128] = fst[
                pl.ds(4 * j + 2 * (1 - mp) + c, HALF, stride=16), :
            ].astype(BF16)
    send(x_send, z_full.at[:, mp], ssem.at[6], rsem.at[6], twin)
    for j in range(CAP):
        for c in range(2):
            z_full[j, mp, :, c * 128 : (c + 1) * 128] = fst[
                pl.ds(4 * j + 2 * mp + c, HALF, stride=16), :
            ].astype(BF16)

    wait_bytes(xx_recv, rsem.at[5])
    own = gw[pl.ds(pl.multiple_of(x * 32, 32), 32), :]
    for d in range(NX - 1):
        own += xx_recv[d].astype(F32)
    for zz in range(NZ):
        for c in range(6):
            zz_send[zz, 4 * c : 4 * c + 4, :] = own[4 * zz : 4 * zz + 4, c * 128 : (c + 1) * 128]
    for d in range(1, NZ):
        zz = lax.rem(z + d, NZ)
        send(zz_send.at[zz], zz_recv.at[d], ssem.at[7], rsem.at[7], (plane * NZ + zz, mp))
    zz_recv[0] = zz_send[z]

    loads[1].wait()
    wait_bytes(e_recv, rsem.at[1])
    wait_bytes(x_send, rsem.at[6])
    far = z_full[...].reshape(CAP * NG, W)
    chunk = 256

    @pl.loop(0, ROWS // chunk)
    def _(i):
        base = pl.multiple_of(i * chunk, chunk)
        row = iota((chunk, NG), 0) + base
        scatter = jnp.concatenate(
            [onehot(row == asked_ref[j : j + 1, :]) for j in range(CAP)], 1
        )
        rows = pl.ds(base, chunk)
        nodes_out[rows, :] = (
            mine[rows, :] + e_recv[rows, :].astype(F32) + dot(scatter, far)
        ).astype(BF16)

    wait_bytes(zz_recv.at[pl.ds(0, NZ - 1)], rsem.at[7])
    final = zz_recv[0]
    for d in range(1, NZ):
        final += zz_recv[d]
    for r in range(4):
        for c in range(6):
            weights_out[r, c // 2 : c // 2 + 1, (c % 2) * 128 : (c % 2 + 1) * 128] = final[
                4 * c + r : 4 * c + r + 1, :
            ]

    wait_bytes(t_ref, ssem.at[0])
    wait_bytes(e_recv, ssem.at[1])
    wait_bytes(y_recv, ssem.at[2])
    wait_bytes(z_recv.at[pl.ds(0, HALF - 1)], ssem.at[3])
    wait_bytes(xx_recv, ssem.at[5])
    wait_bytes(x_send, ssem.at[6])
    wait_bytes(zz_recv.at[pl.ds(0, NZ - 1)], ssem.at[7])


VM = pl.BlockSpec(memory_space=pltpu.VMEM)
ANY = pl.BlockSpec(memory_space=pl.ANY)
LIMIT = 50 * 1024 * 1024


def on_device(
    nodes_in, query, keys, values, grad_attn, w_query, w_key, w_value, halo_owner, halo_row, pattern
):
    owner_r = halo_owner.reshape(1, HR)
    row_r = halo_row.reshape(1, HR)
    dma = pltpu.SemaphoreType.DMA
    halo, far_nodes, asked = pl.pallas_call(
        gather_kernel,
        out_shape=(
            jax.ShapeDtypeStruct((HR, 2 * W), BF16),
            jax.ShapeDtypeStruct((HR, 2 * W), BF16),
            jax.ShapeDtypeStruct((8, 128), I32),
        ),
        in_specs=[VM, VM, VM, ANY, ANY, ANY],
        out_specs=(VM, VM, VM),
        scratch_shapes=[
            pltpu.VMEM((ROWS, W), BF16),
            pltpu.VMEM((ROWS, W), BF16),
            pltpu.VMEM((ROWS, 2 * W), BF16),
            pltpu.VMEM((NZ, 8, 128), I32),
            pltpu.VMEM((NZ, 8, 128), I32),
            pltpu.VMEM((8, 128), I32),
            pltpu.VMEM((NPLANE, 8, 128), I32),
            pltpu.VMEM((NG * 16, 128), F32),
            pltpu.VMEM((NG, 16, 128), BF16),
            pltpu.VMEM((NG, 16, 128), BF16),
            pltpu.VMEM((NG, 16, 128), BF16),
            pltpu.VMEM((HALF, 16, 128), BF16),
            pltpu.VMEM((CAP * NG, 2 * W), BF16),
            pltpu.VMEM((HR, 2 * W), BF16),
            dma((3,)),
            dma((6,)),
            dma((6,)),
        ],
        compiler_params=pltpu.CompilerParams(
            collective_id=0, has_side_effects=True, vmem_limit_bytes=LIMIT
        ),
        name="gather",
    )(halo_owner, owner_r, row_r, keys, values, nodes_in)

    pair = lambda i: (i, 0)
    whole = lambda i: (0, 0)
    steps = ROWS // (2 * BLK)
    t_part, gw, mine, other = pl.pallas_call(
        attention_kernel,
        grid=(steps,),
        out_shape=(
            jax.ShapeDtypeStruct((HR, 2 * W), BF16),
            jax.ShapeDtypeStruct((2 * W, 3 * W), F32),
            jax.ShapeDtypeStruct((ROWS, W), F32),
            jax.ShapeDtypeStruct((ROWS, W), BF16),
        ),
        in_specs=[
            pl.BlockSpec(memory_space=pltpu.SMEM),
            pl.BlockSpec((2 * BLK, W), pair),
            pl.BlockSpec((2 * BLK, W), pair),
            pl.BlockSpec((2 * BLK, W), pair),
            pl.BlockSpec((2 * BLK, W), pair),
            pl.BlockSpec((2 * BLK, 2 * W), pair),
            pl.BlockSpec((HR, 2 * W), whole),
            pl.BlockSpec((HR, 2 * W), whole),
            pl.BlockSpec((2 * W, W), whole),
            pl.BlockSpec((2 * W, W), whole),
            pl.BlockSpec((2 * W, W), whole),
        ],
        out_specs=(
            pl.BlockSpec((HR, 2 * W), whole),
            pl.BlockSpec((2 * W, 3 * W), whole),
            pl.BlockSpec((2 * BLK, W), pair),
            pl.BlockSpec((2 * BLK, W), pair),
        ),
        scratch_shapes=[pltpu.VMEM((W, HR), BF16), pltpu.VMEM((HR, 2 * W), F32)],
        compiler_params=pltpu.CompilerParams(vmem_limit_bytes=LIMIT),
        name="attention",
    )(pattern, query, keys, values, grad_attn, nodes_in, halo, far_nodes, w_query, w_key, w_value)

    return pl.pallas_call(
        return_kernel,
        out_shape=(
            jax.ShapeDtypeStruct((ROWS, W), BF16),
            jax.ShapeDtypeStruct((4, 3, W), F32),
        ),
        in_specs=[VM, VM, VM, VM, ANY, ANY, ANY],
        out_specs=(VM, VM),
        scratch_shapes=[
            pltpu.VMEM((2 * W, 3 * W), F32),
            pltpu.VMEM((ROWS, W), F32),
            pltpu.VMEM((ROWS, W), BF16),
            pltpu.VMEM((HR, 2 * W), BF16),
            pltpu.VMEM((HALF * 16, 128), F32),
            pltpu.VMEM((HALF, 16, 128), BF16),
            pltpu.VMEM((HALF, 16, 128), BF16),
            pltpu.VMEM((CAP, HALF, W), BF16),
            pltpu.VMEM((CAP, 2, HALF, W), BF16),
            pltpu.VMEM((NY, 128, 3 * W), BF16),
            pltpu.VMEM((NY - 1, 128, 3 * W), BF16),
            pltpu.VMEM((NX, 32, 3 * W), BF16),
            pltpu.VMEM((NX - 1, 32, 3 * W), BF16),
            pltpu.VMEM((NZ, 24, 128), F32),
            pltpu.VMEM((NZ, 24, 128), F32),
            dma((2,)),
            dma((8,)),
            dma((8,)),
        ],
        compiler_params=pltpu.CompilerParams(
            collective_id=1, has_side_effects=True, vmem_limit_bytes=LIMIT
        ),
        name="give_back",
    )(halo_owner, owner_r, asked, t_part, gw, mine, other)


def solution(mesh):
    in_specs = (
        P("graph", None),
        P("graph", "mp"),
        P("graph", "mp"),
        P("graph", "mp"),
        P("graph", "mp"),
        P(None, "mp"),
        P(None, "mp"),
        P(None, "mp"),
        P("graph", None),
        P("graph"),
        P("graph", None),
    )
    out_specs = (P("graph", "mp"), P("graph", None, "mp"))
    return jax.shard_map(
        on_device, mesh=mesh, in_specs=in_specs, out_specs=out_specs, check_vma=False
    )
```

```python
import functools
import math

import jax
import jax.numpy as jnp
from jax import lax
from jax.experimental import pallas as pl
from jax.experimental.pallas import tpu as pltpu
from jax.sharding import PartitionSpec as P

MESH = pl.DeviceIdType.MESH
F32 = jnp.float32
BF16 = jnp.bfloat16
I32 = jnp.int32

HEADS_LOCAL = 4
E = 64
BLK = 128
ROWS = 2048
W = 256
HR = 256
CAP = 4
NX, NY, NZ = 4, 4, 8
NG = NX * NY * NZ
NPLANE = NX * NY
HALF = NG // 2
LOG2E = 1.4426950408889634
NT = (((1,), (1,)), ((), ()))
TN = (((0,), (0,)), ((), ()))


def dot(a, b, dims=(((1,), (0,)), ((), ()))):
    return lax.dot_general(a, b, dims, preferred_element_type=F32)


def iota(shape, dim):
    return lax.broadcasted_iota(I32, shape, dim)


def place():
    me = lax.axis_index("graph")
    mp = lax.axis_index("mp")
    return me, mp, lax.div(me, NZ), lax.rem(me, NZ)


def peer(plane, z, dplane, dz):
    return lax.rem(plane + dplane, NPLANE) * NZ + lax.rem(z + dz, NZ)


def relative(owner, plane, z):
    dplane = ((owner >> 3) - plane + NPLANE) & (NPLANE - 1)
    dz = ((owner & 7) - z + NZ) & (NZ - 1)
    return dplane, dz


def rank_column(owner_c, owner_r):
    same = (owner_c == owner_r) & (iota((HR, HR), 1) < iota((HR, HR), 0))
    return jnp.sum(jnp.where(same, 1, 0), axis=1, keepdims=True)


def rank_row(owner_c, owner_r):
    same = (owner_c == owner_r) & (iota((HR, HR), 0) < iota((HR, HR), 1))
    return jnp.sum(jnp.where(same, 1, 0), axis=0, keepdims=True)


def onehot(mask):
    return jnp.where(mask, 1.0, 0.0).astype(BF16)


def wait_bytes(ref, sem):
    pltpu.make_async_copy(ref, ref, sem).wait()


def send(src, dst, ssem, rsem, dev):
    pltpu.make_async_remote_copy(
        src_ref=src, dst_ref=dst, send_sem=ssem, recv_sem=rsem, device_id=dev, device_id_type=MESH
    ).start()


def head_stack(x):
    head_of_lane = iota((BLK, W), 1) // E
    return jnp.concatenate(
        [jnp.where(head_of_lane == h, x, 0.0).astype(BF16) for h in range(HEADS_LOCAL)], 0
    )


def layer_kernel(
    pattern_ref, owner_ref, row_ref,
    query_hbm, keys_hbm, values_hbm, grad_hbm, nodes_hbm, wq_hbm, wk_hbm, wv_hbm,
    nodes_out, weights_out,
    qbuf, kbuf, vbuf, gbuf, nbuf, wbuf, obuf,
    s1, r1, s2, r2, fst, kv_send, kv_recv, n_send, n_recv, stack, fn_send, fn_recv,
    asked_ref, far_kv, far_kt, far_acc, pbuf, dbuf, stats, gw, mine, e_send, e_recv,
    t_send, t_recv, fst2, z_send, z_recv, x_send, z_full,
    y_send, y_recv, xx_send, xx_recv, zz_send, zz_recv,
    lsem, osem, ssem, rsem,
):
    me, mp, plane, z = place()
    y, x = lax.div(plane, NX), lax.rem(plane, NX)
    twin = (me, 1 - mp)
    loads = [
        pltpu.make_async_copy(src, dst, lsem.at[i])
        for i, (src, dst) in enumerate(
            (
                (keys_hbm, kbuf),
                (values_hbm, vbuf),
                (query_hbm, qbuf),
                (grad_hbm, gbuf),
                (nodes_hbm, nbuf),
                (wq_hbm, wbuf.at[0]),
                (wk_hbm, wbuf.at[1]),
                (wv_hbm, wbuf.at[2]),
            )
        )
    ]
    for load in loads:
        load.start()
    z_up = [lax.rem(z + d, NZ) for d in range(NZ)]
    z_down = [lax.rem(z - d + NZ, NZ) for d in range(NZ)]

    barrier = pltpu.get_barrier_semaphore()
    for d in range(1, NZ):
        pl.semaphore_signal(barrier, inc=1, device_id=(plane * NZ + z_up[d], mp), device_id_type=MESH)
    for d in range(1, NPLANE):
        pl.semaphore_signal(barrier, inc=1, device_id=(peer(plane, z, d, 0), mp), device_id_type=MESH)
    pl.semaphore_signal(barrier, inc=1, device_id=twin, device_id_type=MESH)

    owner_r, row_r = owner_ref[...], row_ref[...]
    owner_c = jnp.broadcast_to(owner_r, (HR, HR)).T
    rank_c = rank_column(owner_c, owner_r)
    rank_r = rank_row(owner_c, owner_r)
    dplane_c, dz_c = relative(owner_c[:, 0:1], plane, z)
    dplane_r, dz_r = relative(owner_r, plane, z)
    column = onehot(dplane_c * CAP + rank_c == iota((HR, 128), 1))
    value = row_r + 1
    at_z = dz_r == iota((NZ, HR), 0)
    high = jnp.where(at_z, value >> 6, 0).astype(F32).astype(BF16)
    low = jnp.where(at_z, value & 63, 0).astype(F32).astype(BF16)
    wanted = (dot(high, column) * 64.0 + dot(low, column)).astype(I32) - 1
    for dz in range(NZ):
        s1[dz] = jnp.broadcast_to(wanted[dz : dz + 1, :], (8, 128))
    k_c = dplane_c * NZ + dz_c
    k_r = dplane_r * NZ + dz_r
    pl.semaphore_wait(barrier, NZ - 1 + NPLANE - 1 + 1)

    for dz in range(1, NZ):
        send(s1.at[dz], r1.at[dz], ssem.at[0], rsem.at[0], (plane * NZ + z_up[dz], mp))
    r1[0] = s1[0]
    wait_bytes(r1.at[pl.ds(0, NZ - 1)], rsem.at[0])
    sub = iota((8, 128), 0)
    gathered = jnp.zeros((8, 128), I32)
    for dz in range(NZ):
        gathered = jnp.where(sub == dz, r1[dz], gathered)
    s2[...] = gathered
    for dp in range(1, NPLANE):
        send(s2, r2.at[dp], ssem.at[1], rsem.at[1], (peer(plane, z, dp, 0), mp))
    r2[0] = gathered
    wait_bytes(r2.at[pl.ds(0, NPLANE - 1)], rsem.at[1])

    table = r2[...].reshape(NG, 128)
    table_t = table.T
    lanes, subs = iota((NG, 128), 1), iota((NG, 128), 0)
    asked = []
    for j in range(CAP):
        asked.append(
            jnp.sum(jnp.where(lanes == (subs >> 3) * CAP + j, table, 0), axis=1, keepdims=True)
        )
        asked_ref[j : j + 1, :] = jnp.sum(
            jnp.where(subs == (lanes >> 3) * CAP + j, table_t, 0), axis=0, keepdims=True
        )

    loads[0].wait()
    loads[1].wait()
    for j in range(CAP):
        pick = onehot(asked[j] == iota((NG, ROWS), 1))
        part_k = dot(pick, kbuf[...])
        part_v = dot(pick, vbuf[...])
        for c in range(2):
            fst[pl.ds(4 * j + c, NG, stride=16), :] = part_k[:, c * 128 : (c + 1) * 128]
            fst[pl.ds(4 * j + 2 + c, NG, stride=16), :] = part_v[:, c * 128 : (c + 1) * 128]
    kv_send[...] = fst[...].reshape(NG, 16, 128).astype(BF16)

    @pl.loop(0, NPLANE)
    def _(dp):
        base = lax.rem(plane - dp + NPLANE, NPLANE) * NZ
        for dz in range(1, NZ):
            k = dp * NZ + dz
            send(kv_send.at[k], kv_recv.at[k], ssem.at[2], rsem.at[2], (base + z_down[dz], mp))

    @pl.loop(1, NPLANE)
    def _(dp):
        base = lax.rem(plane - dp + NPLANE, NPLANE) * NZ
        send(kv_send.at[dp * NZ], kv_recv.at[dp * NZ], ssem.at[2], rsem.at[2], (base + z, mp))

    kv_recv[0] = kv_send[0]

    for load in loads[2:]:
        load.wait()

    @pl.loop(0, ROWS // (2 * BLK))
    def _(step):
        for half in range(2):
            b = 2 * step + half
            rows = pl.ds(pl.multiple_of(b * BLK, BLK), BLK)
            qm = head_stack(qbuf[rows, :] * 0.125)
            gm = head_stack(gbuf[rows, :])
            s_own = dot(kbuf[rows, :], qm, NT)
            d_own = dot(vbuf[rows, :], gm, NT)
            top = jnp.max(s_own, 0, keepdims=True)
            p_own = jnp.exp2((s_own - top) * LOG2E)
            pbuf[rows, :] = p_own
            dbuf[rows, :] = d_own
            stats[b, 0:1, :] = top
            stats[b, 1:2, :] = jnp.sum(p_own, 0, keepdims=True)
            stats[b, 2:3, :] = jnp.sum(p_own * d_own, 0, keepdims=True)

    for j in range(CAP):
        pick = onehot(asked[j] == iota((NG, ROWS), 1))
        part_n = dot(pick, nbuf[...])
        for c in range(4):
            fst[pl.ds(4 * j + c, NG, stride=16), :] = part_n[:, c * 128 : (c + 1) * 128]
    n_send[...] = fst[...].reshape(NG, 16, 128).astype(BF16)
    gw[...] = jnp.zeros_like(gw)
    far_acc[...] = jnp.zeros_like(far_acc)

    wait_bytes(kv_recv.at[pl.ds(0, NG - 1)], rsem.at[2])
    fst[...] = kv_recv[...].astype(F32).reshape(NG * 16, 128)
    for j in range(CAP):
        for c in range(4):
            stack[j * NG : (j + 1) * NG, c * 128 : (c + 1) * 128] = fst[
                pl.ds(4 * j + c, NG, stride=16), :
            ].astype(BF16)
    place_mat = onehot(rank_c * NG + k_c == iota((HR, CAP * NG), 1))
    far_kv[...] = dot(place_mat, stack[...]).astype(BF16)
    far_kt[...] = (far_kv[:, 0:W] * 0.125).T

    mine_rows = pl.ds(pl.multiple_of(mp * W, W), W)
    other_rows = pl.ds(pl.multiple_of((1 - mp) * W, W), W)

    def attend(step):
        far_k = far_kv[:, 0:W]
        far_v = far_kv[:, W : 2 * W]
        slopes_far, lows_far, queries, grads = [], [], [], []
        for half in range(2):
            b = 2 * step + half
            rows = pl.ds(pl.multiple_of(b * BLK, BLK), BLK)
            qm = head_stack(qbuf[rows, :] * 0.125)
            gm = head_stack(gbuf[rows, :])
            bias = [jnp.where(pattern_ref[h, b] > 0, 0.0, 1e30).astype(F32) for h in range(2)]
            s_far = dot(far_k, qm, NT)
            d_far = dot(far_v, gm, NT)
            top_own = stats[b, 0:1, :]
            top = jnp.maximum(
                top_own,
                jnp.maximum(
                    jnp.max(s_far[0:BLK], 0, keepdims=True) - bias[0],
                    jnp.max(s_far[BLK:], 0, keepdims=True) - bias[1],
                ),
            )
            p_far = jnp.concatenate(
                [
                    jnp.exp2((s_far[0:BLK] - (top + bias[0])) * LOG2E),
                    jnp.exp2((s_far[BLK:] - (top + bias[1])) * LOG2E),
                ],
                0,
            )
            share = jnp.exp2((top_own - top) * LOG2E)
            inv = 1.0 / (stats[b, 1:2, :] * share + jnp.sum(p_far, 0, keepdims=True))
            term = (stats[b, 2:3, :] * share + jnp.sum(p_far * d_far, 0, keepdims=True)) * inv
            prob_own = pbuf[rows, :] * (share * inv)
            prob_far = p_far * inv
            slope_own = (prob_own * (dbuf[rows, :] - term)).astype(BF16)
            slope_far = (prob_far * (d_far - term)).astype(BF16)
            low_own = prob_own.astype(BF16)
            low_far = prob_far.astype(BF16)
            dk = dot(slope_own, qm)
            dv = dot(low_own, gm)
            kt = (kbuf[rows, :] * 0.125).T
            dqt = jnp.concatenate(
                [
                    dot(kt[h * E : (h + 1) * E, :], slope_own[:, h * BLK : (h + 1) * BLK])
                    + dot(far_kt[h * E : (h + 1) * E, :], slope_far[:, h * BLK : (h + 1) * BLK])
                    for h in range(HEADS_LOCAL)
                ],
                0,
            )
            grads.append((dqt.T.astype(BF16), dk.astype(BF16), dv.astype(BF16)))
            slopes_far.append(slope_far)
            lows_far.append(low_far)
            queries.append((qm, gm))

        far_acc[:, 0:W] += dot(
            jnp.concatenate(slopes_far, 1), jnp.concatenate([a for a, _ in queries], 0)
        )
        far_acc[:, W : 2 * W] += dot(
            jnp.concatenate(lows_far, 1), jnp.concatenate([a for _, a in queries], 0)
        )
        rows = pl.ds(pl.multiple_of(step * 2 * BLK, 2 * BLK), 2 * BLK)
        nodes = nbuf[rows, :]
        kept = jnp.zeros((2 * BLK, W), F32)
        given = jnp.zeros((2 * BLK, W), F32)
        for i in range(3):
            grad = jnp.concatenate([grads[0][i], grads[1][i]], 0)
            gw[:, i * W : (i + 1) * W] += dot(nodes, grad, TN)
            kept += dot(grad, wbuf[i, mine_rows, :], NT)
            given += dot(grad, wbuf[i, other_rows, :], NT)
        mine[rows, :] = kept
        e_send[rows, :] = given.astype(BF16)
        send(e_send.at[rows], e_recv.at[rows], ssem.at[6], rsem.at[6], twin)

    first_plane = mp * (NPLANE // 2)

    def send_nodes(i):
        dp = first_plane + i
        base = lax.rem(plane - dp + NPLANE, NPLANE) * NZ
        for dz in range(1, NZ):
            k = i * NZ + dz
            send(
                n_send.at[dp * NZ + dz], n_recv.at[k], ssem.at[3], rsem.at[3],
                (base + z_down[dz], mp),
            )

    @pl.loop(1, NPLANE // 2)
    def _(i):
        dp = first_plane + i
        base = lax.rem(plane - dp + NPLANE, NPLANE) * NZ
        send(n_send.at[dp * NZ], n_recv.at[i * NZ], ssem.at[3], rsem.at[3], (base + z, mp))

    @pl.when(mp == 1)
    def _():
        base = lax.rem(plane + NPLANE // 2, NPLANE) * NZ
        send(n_send.at[HALF], n_recv.at[0], ssem.at[4], rsem.at[4], (base + z, mp))

    @pl.when(mp == 0)
    def _():
        n_recv[0] = n_send[0]

    steps = ROWS // (2 * BLK)
    early = steps // 2

    @pl.loop(0, early)
    def _(step):
        send_nodes(2 * step)
        send_nodes(2 * step + 1)
        attend(step)

    k_ch = k_c - mp * HALF
    slot_c = jnp.where((k_ch >= 0) & (k_ch < HALF), rank_c * HALF + k_ch, -1)
    k_rh = k_r - mp * HALF
    slot_r = jnp.where((k_rh >= 0) & (k_rh < HALF), rank_r * HALF + k_rh, -1)
    wait_bytes(n_recv.at[pl.ds(0, HALF - 1)], rsem.at[3])

    @pl.when(mp == 1)
    def _():
        wait_bytes(n_recv.at[0], rsem.at[4])

    fst[0 : HALF * 16, :] = n_recv[...].astype(F32).reshape(HALF * 16, 128)
    for j in range(CAP):
        for c in range(4):
            stack[j * HALF : (j + 1) * HALF, c * 128 : (c + 1) * 128] = fst[
                pl.ds(4 * j + c, HALF, stride=16), :
            ].astype(BF16)
    place_half = onehot(slot_c == iota((HR, CAP * HALF), 1))
    fn_send[...] = dot(place_half, stack[0 : CAP * HALF, :]).astype(BF16)
    send(fn_send, fn_recv, ssem.at[5], rsem.at[5], twin)

    @pl.loop(early, steps)
    def _(step):
        attend(step)

    dk_far = far_acc[:, 0:W].astype(BF16)
    dv_far = far_acc[:, W : 2 * W].astype(BF16)
    t_send[...] = (dot(dk_far, wbuf[1], NT) + dot(dv_far, wbuf[2], NT)).astype(BF16)
    send(t_send, t_recv, ssem.at[7], rsem.at[7], twin)
    wait_bytes(fn_recv, rsem.at[5])
    far_nodes = fn_send[...] + fn_recv[...]
    gw[:, W : 2 * W] += dot(far_nodes, dk_far, TN)
    gw[:, 2 * W : 3 * W] += dot(far_nodes, dv_far, TN)
    y_send[...] = gw[...].astype(BF16).reshape(NY, 128, 3 * W)
    for d in range(1, NY):
        yy = lax.rem(y + d, NY)
        send(y_send.at[yy], y_recv.at[d - 1], ssem.at[8], rsem.at[8], ((yy * NX + x) * NZ + z, mp))

    place_t = onehot(slot_r == iota((CAP * HALF, HR), 0))
    wait_bytes(t_recv, rsem.at[7])
    summed = (t_send[...].astype(F32) + t_recv[...].astype(F32)).astype(BF16)
    placed = dot(place_t, summed)
    for j in range(CAP):
        for c in range(4):
            fst2[pl.ds(4 * j + c, HALF, stride=16), :] = placed[
                j * HALF : (j + 1) * HALF, c * 128 : (c + 1) * 128
            ]
    z_send[...] = fst2[...].reshape(HALF, 16, 128).astype(BF16)

    @pl.loop(0, NPLANE // 2)
    def _(i):
        base = lax.rem(plane + first_plane + i, NPLANE) * NZ
        for dz in range(1, NZ):
            k = i * NZ + dz
            send(z_send.at[k], z_recv.at[k], ssem.at[9], rsem.at[9], (base + z_up[dz], mp))

    @pl.loop(1, NPLANE // 2)
    def _(i):
        base = lax.rem(plane + first_plane + i, NPLANE) * NZ
        send(z_send.at[i * NZ], z_recv.at[i * NZ], ssem.at[9], rsem.at[9], (base + z, mp))

    @pl.when(mp == 1)
    def _():
        base = lax.rem(plane + NPLANE // 2, NPLANE) * NZ
        send(z_send.at[0], z_recv.at[0], ssem.at[10], rsem.at[10], (base + z, mp))

    @pl.when(mp == 0)
    def _():
        z_recv[0] = z_send[0]

    wait_bytes(y_recv, rsem.at[8])
    own = gw[pl.ds(pl.multiple_of(y * 128, 128), 128), :]
    for d in range(NY - 1):
        own += y_recv[d].astype(F32)
    gw[0:128, :] = own
    xx_send[...] = own.astype(BF16).reshape(NX, 32, 3 * W)
    for d in range(1, NX):
        xx = lax.rem(x + d, NX)
        send(xx_send.at[xx], xx_recv.at[d - 1], ssem.at[11], rsem.at[11], ((y * NX + xx) * NZ + z, mp))
    wait_bytes(xx_recv, rsem.at[11])
    own = gw[pl.ds(pl.multiple_of(x * 32, 32), 32), :]
    for d in range(NX - 1):
        own += xx_recv[d].astype(F32)
    for zz in range(NZ):
        for c in range(6):
            zz_send[zz, 4 * c : 4 * c + 4, :] = own[4 * zz : 4 * zz + 4, c * 128 : (c + 1) * 128]
    for d in range(1, NZ):
        send(
            zz_send.at[z_up[d]], zz_recv.at[d], ssem.at[12], rsem.at[12], (plane * NZ + z_up[d], mp)
        )
    zz_recv[0] = zz_send[z]

    wait_bytes(z_recv.at[pl.ds(0, HALF - 1)], rsem.at[9])

    @pl.when(mp == 1)
    def _():
        wait_bytes(z_recv.at[0], rsem.at[10])

    fst2[...] = z_recv[...].astype(F32).reshape(HALF * 16, 128)
    for j in range(CAP):
        for c in range(2):
            x_send[j, :, c * 128 : (c + 1) * 128] = fst2[
                pl.ds(4 * j + 2 * (1 - mp) + c, HALF, stride=16), :
            ].astype(BF16)
    send(x_send, z_full.at[:, mp], ssem.at[13], rsem.at[13], twin)
    for j in range(CAP):
        for c in range(2):
            z_full[j, mp, :, c * 128 : (c + 1) * 128] = fst2[
                pl.ds(4 * j + 2 * mp + c, HALF, stride=16), :
            ].astype(BF16)

    wait_bytes(zz_recv.at[pl.ds(0, NZ - 1)], rsem.at[12])
    final = zz_recv[0]
    for d in range(1, NZ):
        final += zz_recv[d]
    for r in range(4):
        for c in range(6):
            weights_out[r, c // 2 : c // 2 + 1, (c % 2) * 128 : (c % 2 + 1) * 128] = final[
                4 * c + r : 4 * c + r + 1, :
            ]

    wait_bytes(e_recv, rsem.at[6])
    wait_bytes(x_send, rsem.at[13])
    far = z_full[...].reshape(CAP * NG, W)
    chunk = 256

    @pl.loop(0, ROWS // chunk)
    def _(i):
        base = pl.multiple_of(i * chunk, chunk)
        row = iota((chunk, NG), 0) + base
        scatter = jnp.concatenate(
            [onehot(row == asked_ref[j : j + 1, :]) for j in range(CAP)], 1
        )
        rows = pl.ds(base, chunk)
        obuf[rows, :] = (
            mine[rows, :] + e_recv[rows, :].astype(F32) + dot(scatter, far)
        ).astype(BF16)
        pltpu.make_async_copy(obuf.at[rows], nodes_out.at[rows], osem).start()

    wait_bytes(s1.at[pl.ds(0, NZ - 1)], ssem.at[0])
    wait_bytes(r2.at[pl.ds(0, NPLANE - 1)], ssem.at[1])
    wait_bytes(kv_send.at[pl.ds(0, NG - 1)], ssem.at[2])
    wait_bytes(n_recv.at[pl.ds(0, HALF - 1)], ssem.at[3])
    wait_bytes(fn_recv, ssem.at[5])
    wait_bytes(e_recv, ssem.at[6])
    wait_bytes(t_recv, ssem.at[7])
    wait_bytes(y_recv, ssem.at[8])
    wait_bytes(z_recv.at[pl.ds(0, HALF - 1)], ssem.at[9])
    wait_bytes(xx_recv, ssem.at[11])
    wait_bytes(zz_recv.at[pl.ds(0, NZ - 1)], ssem.at[12])
    wait_bytes(x_send, ssem.at[13])

    @pl.when(mp == 1)
    def _():
        wait_bytes(n_recv.at[0], ssem.at[4])
        wait_bytes(z_recv.at[0], ssem.at[10])

    wait_bytes(obuf, osem)


VM = pl.BlockSpec(memory_space=pltpu.VMEM)
ANY = pl.BlockSpec(memory_space=pl.ANY)
LIMIT = 56 * 1024 * 1024


def on_device(
    nodes_in, query, keys, values, grad_attn, w_query, w_key, w_value, halo_owner, halo_row, pattern
):
    dma = pltpu.SemaphoreType.DMA
    vm = pltpu.VMEM
    return pl.pallas_call(
        layer_kernel,
        out_shape=(
            jax.ShapeDtypeStruct((ROWS, W), BF16),
            jax.ShapeDtypeStruct((4, 3, W), F32),
        ),
        in_specs=[pl.BlockSpec(memory_space=pltpu.SMEM), VM, VM] + [ANY] * 8,
        out_specs=(ANY, VM),
        scratch_shapes=[
            vm((ROWS, W), BF16),
            vm((ROWS, W), BF16),
            vm((ROWS, W), BF16),
            vm((ROWS, W), BF16),
            vm((ROWS, 2 * W), BF16),
            vm((3, 2 * W, W), BF16),
            vm((ROWS, W), BF16),
            vm((NZ, 8, 128), I32),
            vm((NZ, 8, 128), I32),
            vm((8, 128), I32),
            vm((NPLANE, 8, 128), I32),
            vm((NG * 16, 128), F32),
            vm((NG, 16, 128), BF16),
            vm((NG, 16, 128), BF16),
            vm((NG, 16, 128), BF16),
            vm((HALF, 16, 128), BF16),
            vm((CAP * NG, 2 * W), BF16),
            vm((HR, 2 * W), BF16),
            vm((HR, 2 * W), BF16),
            vm((8, 128), I32),
            vm((HR, 2 * W), BF16),
            vm((W, HR), BF16),
            vm((HR, 2 * W), F32),
            vm((ROWS, HEADS_LOCAL * BLK), F32),
            vm((ROWS, HEADS_LOCAL * BLK), F32),
            vm((ROWS // BLK, 8, HEADS_LOCAL * BLK), F32),
            vm((2 * W, 3 * W), F32),
            vm((ROWS, W), F32),
            vm((ROWS, W), BF16),
            vm((ROWS, W), BF16),
            vm((HR, 2 * W), BF16),
            vm((HR, 2 * W), BF16),
            vm((HALF * 16, 128), F32),
            vm((HALF, 16, 128), BF16),
            vm((HALF, 16, 128), BF16),
            vm((CAP, HALF, W), BF16),
            vm((CAP, 2, HALF, W), BF16),
            vm((NY, 128, 3 * W), BF16),
            vm((NY - 1, 128, 3 * W), BF16),
            vm((NX, 32, 3 * W), BF16),
            vm((NX - 1, 32, 3 * W), BF16),
            vm((NZ, 24, 128), F32),
            vm((NZ, 24, 128), F32),
            dma((8,)),
            dma,
            dma((14,)),
            dma((14,)),
        ],
        compiler_params=pltpu.CompilerParams(
            collective_id=0, has_side_effects=True, vmem_limit_bytes=LIMIT
        ),
        name="layer",
    )(
        pattern.T, halo_owner.reshape(1, HR), halo_row.reshape(1, HR),
        query, keys, values, grad_attn, nodes_in, w_query, w_key, w_value,
    )


def solution(mesh):
    in_specs = (
        P("graph", None),
        P("graph", "mp"),
        P("graph", "mp"),
        P("graph", "mp"),
        P("graph", "mp"),
        P(None, "mp"),
        P(None, "mp"),
        P(None, "mp"),
        P("graph", None),
        P("graph"),
        P("graph", None),
    )
    out_specs = (P("graph", "mp"), P("graph", None, "mp"))
    return jax.shard_map(
        on_device, mesh=mesh, in_specs=in_specs, out_specs=out_specs, check_vma=False
    )
```

```python
import functools
import math

import jax
import jax.numpy as jnp
from jax import lax
from jax.experimental import pallas as pl
from jax.experimental.pallas import tpu as pltpu
from jax.sharding import PartitionSpec as P

MESH = pl.DeviceIdType.MESH
F32 = jnp.float32
BF16 = jnp.bfloat16
I32 = jnp.int32

HEADS_LOCAL = 4
E = 64
BLK = 128
ROWS = 2048
W = 256
HR = 256
CAP = 4
NX, NY, NZ = 4, 4, 8
NG = NX * NY * NZ
NPLANE = NX * NY
HALF = NG // 2
LOG2E = 1.4426950408889634
NT = (((1,), (1,)), ((), ()))
TN = (((0,), (0,)), ((), ()))


def dot(a, b, dims=(((1,), (0,)), ((), ()))):
    return lax.dot_general(a, b, dims, preferred_element_type=F32)


def iota(shape, dim):
    return lax.broadcasted_iota(I32, shape, dim)


def place():
    me = lax.axis_index("graph")
    mp = lax.axis_index("mp")
    return me, mp, lax.div(me, NZ), lax.rem(me, NZ)


def peer(plane, z, dplane, dz):
    return lax.rem(plane + dplane, NPLANE) * NZ + lax.rem(z + dz, NZ)


def relative(owner, plane, z):
    dplane = ((owner >> 3) - plane + NPLANE) & (NPLANE - 1)
    dz = ((owner & 7) - z + NZ) & (NZ - 1)
    return dplane, dz


def rank_column(owner_c, owner_r):
    same = (owner_c == owner_r) & (iota((HR, HR), 1) < iota((HR, HR), 0))
    return jnp.sum(jnp.where(same, 1, 0), axis=1, keepdims=True)


def rank_row(owner_c, owner_r):
    same = (owner_c == owner_r) & (iota((HR, HR), 0) < iota((HR, HR), 1))
    return jnp.sum(jnp.where(same, 1, 0), axis=0, keepdims=True)


def onehot(mask):
    return jnp.where(mask, 1.0, 0.0).astype(BF16)


def wait_bytes(ref, sem):
    pltpu.make_async_copy(ref, ref, sem).wait()


def send(src, dst, ssem, rsem, dev):
    pltpu.make_async_remote_copy(
        src_ref=src, dst_ref=dst, send_sem=ssem, recv_sem=rsem, device_id=dev, device_id_type=MESH
    ).start()


def head_stack(x):
    head_of_lane = iota((2 * BLK, W), 1) // E
    return jnp.concatenate(
        [jnp.where(head_of_lane == h, x, 0.0).astype(BF16) for h in range(HEADS_LOCAL)], 0
    )


def block_rows(x, half):
    return jnp.concatenate(
        [x[(2 * h + half) * BLK : (2 * h + half + 1) * BLK, :] for h in range(HEADS_LOCAL)], 0
    )


def block_lanes(x, half):
    return jnp.concatenate(
        [x[:, (2 * h + half) * BLK : (2 * h + half + 1) * BLK] for h in range(HEADS_LOCAL)], 1
    )


def layer_kernel(
    pattern_hbm, owner_hbm, row_hbm,
    query_hbm, keys_hbm, values_hbm, grad_hbm, nodes_hbm, wq_hbm, wk_hbm, wv_hbm,
    nodes_out, weights_out,
    qbuf, kbuf, vbuf, gbuf, nbuf, wbuf,
    s1, r1, s2, r2, fst, kv_send, kv_recv, n_send, n_recv, stack, fn_send, fn_recv,
    pattern_ref, owner_ref, row_ref, asked_ref, far_kv, far_kt, far_acc, pbuf, dbuf, stats, gw, mine, e_recv,
    qms, gms, kts, ntr, scat, grads, even, odd,
    t_recv, z_send, z_recv, x_send, z_full,
    a_send, a_recv, b_send, b_recv, a_sum, b_sum, a2_send, a2_recv, b2_send, b2_recv,
    zz_send, zz_recv,
    lsem, ssem, rsem,
):
    me, mp, plane, z = place()
    y, x = lax.div(plane, NX), lax.rem(plane, NX)
    twin = (me, 1 - mp)
    loads = [
        pltpu.make_async_copy(src, dst, lsem.at[i])
        for i, (src, dst) in enumerate(
            (
                (keys_hbm, kbuf),
                (values_hbm, vbuf),
                (query_hbm, qbuf),
                (grad_hbm, gbuf),
                (nodes_hbm, nbuf),
                (wq_hbm, wbuf.at[0]),
                (wk_hbm, wbuf.at[1]),
                (wv_hbm, wbuf.at[2]),
                (owner_hbm, owner_ref),
                (row_hbm, row_ref),
                (pattern_hbm, pattern_ref),
            )
        )
    ]
    z_up = [lax.rem(z + d, NZ) for d in range(NZ)]
    z_down = [lax.rem(z - d + NZ, NZ) for d in range(NZ)]

    barrier = pltpu.get_barrier_semaphore()
    for d in range(1, NZ):
        pl.semaphore_signal(barrier, inc=1, device_id=(plane * NZ + z_up[d], mp), device_id_type=MESH)
    for d in range(1, NPLANE):
        pl.semaphore_signal(barrier, inc=1, device_id=(peer(plane, z, d, 0), mp), device_id_type=MESH)
    pl.semaphore_signal(barrier, inc=1, device_id=twin, device_id_type=MESH)

    for load in loads[8:] + loads[0:2]:
        load.start()

    for load in loads[8:]:
        load.wait()
    owner_r, row_r = owner_ref[...], row_ref[...]
    owner_c = jnp.broadcast_to(owner_r, (HR, HR)).T
    rank_c = rank_column(owner_c, owner_r)
    rank_r = rank_row(owner_c, owner_r)
    dplane_c, dz_c = relative(owner_c[:, 0:1], plane, z)
    dplane_r, dz_r = relative(owner_r, plane, z)
    column = onehot(dplane_c * CAP + rank_c == iota((HR, 128), 1))
    value = row_r + 1
    at_z = dz_r == iota((NZ, HR), 0)
    high = jnp.where(at_z, value >> 6, 0).astype(F32).astype(BF16)
    low = jnp.where(at_z, value & 63, 0).astype(F32).astype(BF16)
    wanted = (dot(high, column) * 64.0 + dot(low, column)).astype(I32) - 1
    for dz in range(NZ):
        s1[dz] = wanted[dz : dz + 1, :]
    k_c = dplane_c * NZ + dz_c
    k_r = dplane_r * NZ + dz_r
    pl.semaphore_wait(barrier, NZ - 1 + NPLANE - 1 + 1)

    for dz in range(1, NZ):
        send(s1.at[dz], r1.at[dz], ssem.at[0], rsem.at[0], (plane * NZ + z_up[dz], mp))
    r1[0] = s1[0]
    wait_bytes(r1.at[pl.ds(0, NZ - 1)], rsem.at[0])
    sub = iota((8, 128), 0)
    gathered = jnp.zeros((8, 128), I32)
    for dz in range(NZ):
        gathered = jnp.where(sub == dz, r1[dz], gathered)
    s2[...] = gathered
    for dp in range(1, NPLANE):
        send(s2, r2.at[dp], ssem.at[1], rsem.at[1], (peer(plane, z, dp, 0), mp))
    r2[0] = gathered
    wait_bytes(r2.at[pl.ds(0, NPLANE - 1)], rsem.at[1])

    for load in loads[2:8]:
        load.start()
    table = r2[...].reshape(NG, 128)
    table_t = table.T
    lanes, subs = iota((NG, 128), 1), iota((NG, 128), 0)
    asked = []
    for j in range(CAP):
        asked.append(
            jnp.sum(jnp.where(lanes == (subs >> 3) * CAP + j, table, 0), axis=1, keepdims=True)
        )
        asked_ref[j : j + 1, :] = jnp.sum(
            jnp.where(subs == (lanes >> 3) * CAP + j, table_t, 0), axis=0, keepdims=True
        )

    loads[0].wait()
    loads[1].wait()
    for j in range(CAP):
        pick = onehot(asked[j] == iota((NG, ROWS), 1))
        part_k = dot(pick, kbuf[...])
        part_v = dot(pick, vbuf[...])
        for c in range(2):
            fst[pl.ds(4 * j + c, NG, stride=16), :] = part_k[:, c * 128 : (c + 1) * 128]
            fst[pl.ds(4 * j + 2 + c, NG, stride=16), :] = part_v[:, c * 128 : (c + 1) * 128]
    kv_send[...] = fst[...].reshape(NG, 16, 128).astype(BF16)

    @pl.loop(0, NPLANE)
    def _(dp):
        base = lax.rem(plane - dp + NPLANE, NPLANE) * NZ
        for dz in range(1, NZ):
            k = dp * NZ + dz
            send(kv_send.at[k], kv_recv.at[k], ssem.at[2], rsem.at[2], (base + z_down[dz], mp))

    @pl.loop(1, NPLANE)
    def _(dp):
        base = lax.rem(plane - dp + NPLANE, NPLANE) * NZ
        send(kv_send.at[dp * NZ], kv_recv.at[dp * NZ], ssem.at[2], rsem.at[2], (base + z, mp))

    kv_recv[0] = kv_send[0]

    for load in loads[2:8]:
        load.wait()

    @pl.loop(0, ROWS // (2 * BLK))
    def _(step):
        both = pl.ds(pl.multiple_of(step * 2 * BLK, 2 * BLK), 2 * BLK)
        qm = head_stack(qbuf[both, :] * 0.125)
        gm = head_stack(gbuf[both, :])
        qms[step] = qm
        gms[step] = gm
        kts[step] = (kbuf[both, :] * 0.125).T
        ntr[step] = nbuf[both, :].T
        for half in range(2):
            rows = pl.ds(pl.multiple_of(step * 2 * BLK + half * BLK, BLK), BLK)
            s_own = dot(kbuf[rows, :], block_rows(qm, half), NT)
            d_own = dot(vbuf[rows, :], block_rows(gm, half), NT)
            top = jnp.max(s_own, 0, keepdims=True)
            p_own = jnp.exp2((s_own - top) * LOG2E)
            total = jnp.sum(p_own, 0, keepdims=True)
            term = jnp.sum(p_own * d_own, 0, keepdims=True)
            for h in range(HEADS_LOCAL):
                src = slice(h * BLK, (h + 1) * BLK)
                dst = slice((2 * h + half) * BLK, (2 * h + half + 1) * BLK)
                pbuf[step, :, dst] = p_own[:, src]
                dbuf[step, :, dst] = d_own[:, src]
                stats[step, 0:1, dst] = top[:, src]
                stats[step, 1:2, dst] = total[:, src]
                stats[step, 2:3, dst] = term[:, src]

    for j in range(CAP):
        pick = onehot(asked[j] == iota((NG, ROWS), 1))
        part_n = dot(pick, nbuf[...])
        for c in range(4):
            fst[pl.ds(4 * j + c, NG, stride=16), :] = part_n[:, c * 128 : (c + 1) * 128]
    n_send[...] = fst[...].reshape(NG, 16, 128).astype(BF16)
    far_acc[...] = jnp.zeros_like(far_acc)
    odd[...] = jnp.zeros_like(odd)

    @pl.loop(0, ROWS // 256)
    def _(i):
        base = pl.multiple_of(i * 256, 256)
        row = iota((256, NG), 0) + base
        for j in range(CAP):
            scat[pl.ds(base, 256), j * NG : (j + 1) * NG] = onehot(row == asked_ref[j : j + 1, :])


    wait_bytes(kv_recv.at[pl.ds(0, NG - 1)], rsem.at[2])
    fst[...] = kv_recv[...].astype(F32).reshape(NG * 16, 128)
    for j in range(CAP):
        for c in range(4):
            stack[j * NG : (j + 1) * NG, c * 128 : (c + 1) * 128] = fst[
                pl.ds(4 * j + c, NG, stride=16), :
            ].astype(BF16)
    place_mat = onehot(rank_c * NG + k_c == iota((HR, CAP * NG), 1))
    far_kv[...] = dot(place_mat, stack[...]).astype(BF16)
    far_kt[...] = (far_kv[:, 0:W] * 0.125).T

    mine_rows = pl.ds(pl.multiple_of(mp * W, W), W)
    other_rows = pl.ds(pl.multiple_of((1 - mp) * W, W), W)

    def scores(step, h):
        rows = slice(2 * h * BLK, 2 * (h + 1) * BLK)
        return (
            dot(far_kv[:, 0:W], qms[step, rows, :], NT),
            dot(far_kv[:, W : 2 * W], gms[step, rows, :], NT),
        )

    def soften(step, h, bias, s_far, d_far, buf):
        lanes = slice(2 * h * BLK, 2 * (h + 1) * BLK)
        top_own = stats[step, 0:1, lanes]
        top = jnp.maximum(
            top_own,
            jnp.maximum(
                jnp.max(s_far[0:BLK], 0, keepdims=True) - bias[0],
                jnp.max(s_far[BLK:], 0, keepdims=True) - bias[1],
            ),
        )
        p_far = jnp.concatenate(
            [
                jnp.exp2((s_far[0:BLK] - (top + bias[0])) * LOG2E),
                jnp.exp2((s_far[BLK:] - (top + bias[1])) * LOG2E),
            ],
            0,
        )
        share = jnp.exp2((top_own - top) * LOG2E)
        inv = 1.0 / (stats[step, 1:2, lanes] * share + jnp.sum(p_far, 0, keepdims=True))
        term = (stats[step, 2:3, lanes] * share + jnp.sum(p_far * d_far, 0, keepdims=True)) * inv
        prob_own = pbuf[step, :, lanes] * (share * inv)
        prob_far = p_far * inv
        buf[0, 0:BLK, lanes] = (prob_own * (dbuf[step, :, lanes] - term)).astype(BF16)
        buf[0, BLK:, lanes] = (prob_far * (d_far - term)).astype(BF16)
        buf[1, 0:BLK, lanes] = prob_own.astype(BF16)
        buf[1, BLK:, lanes] = prob_far.astype(BF16)

    def apply(step, buf, part):
        first = pl.multiple_of(step * 2 * BLK, 2 * BLK)
        if part < 2:
            stacked = (qms, gms)[part]
            far_acc[:, part * W : (part + 1) * W] += dot(buf[part, BLK:, :], stacked[step])
        elif part == 2:
            pieces = []
            for h in range(HEADS_LOCAL):
                heads = slice(h * E, (h + 1) * E)
                own_part = [
                    dot(
                        kts[step, heads, half * BLK : (half + 1) * BLK],
                        buf[0, 0:BLK, (2 * h + half) * BLK : (2 * h + half + 1) * BLK],
                    )
                    for half in range(2)
                ]
                pieces.append(
                    dot(far_kt[heads, :], buf[0, BLK:, 2 * h * BLK : 2 * (h + 1) * BLK])
                    + jnp.concatenate(own_part, 1)
                )
            grads[pl.ds(first, 2 * BLK), 0:W] = jnp.concatenate(pieces, 0).T.astype(BF16)
        else:
            for i, stacked in enumerate((qms, gms)):
                for half in range(2):
                    rows = pl.ds(pl.multiple_of(first + half * BLK, BLK), BLK)
                    grads[rows, (i + 1) * W : (i + 2) * W] = dot(
                        block_lanes(buf[i, 0:BLK, :], half), block_rows(stacked[step], half)
                    ).astype(BF16)

    def attend(step, buf, before, buf_before):
        second = ((iota((1, 2 * BLK), 1) >> 7) & 1) == 1
        bias = []
        for h in range(2):
            each = [
                jnp.where(pattern_ref[h, 2 * step + half] > 0, 0.0, 1e30).astype(F32)
                for half in range(2)
            ]
            bias.append(jnp.where(second, each[1], each[0]))
        ready = scores(step, 0)
        for h in range(HEADS_LOCAL):
            now = ready
            if h + 1 < HEADS_LOCAL:
                ready = scores(step, h + 1)
            apply(before, buf_before, h)
            soften(step, h, bias, now[0], now[1], buf)

    def attend_pair(t):
        attend(2 * t, even, jnp.maximum(2 * t - 1, 0), odd)
        attend(2 * t + 1, odd, 2 * t, even)

    def project(step):
        both = pl.ds(pl.multiple_of(step * 2 * BLK, 2 * BLK), 2 * BLK)
        kept = jnp.zeros((2 * BLK, W), F32)
        given = jnp.zeros((2 * BLK, W), F32)
        for i in range(3):
            grad = grads[both, i * W : (i + 1) * W]
            kept += dot(grad, wbuf[i, mine_rows, :], NT)
            given += dot(grad, wbuf[i, other_rows, :], NT)
        mine[both, :] = kept
        gbuf[both, :] = given.astype(BF16)
        send(gbuf.at[both], e_recv.at[both], ssem.at[6], rsem.at[6], twin)

    first_plane = mp * (NPLANE // 2)

    @pl.loop(0, NPLANE // 2)
    def _(i):
        dp = first_plane + i
        base = lax.rem(plane - dp + NPLANE, NPLANE) * NZ
        for dz in range(1, NZ):
            send(
                n_send.at[dp * NZ + dz], n_recv.at[i * NZ + dz], ssem.at[3], rsem.at[3],
                (base + z_down[dz], mp),
            )

    @pl.loop(1, NPLANE // 2)
    def _(i):
        dp = first_plane + i
        base = lax.rem(plane - dp + NPLANE, NPLANE) * NZ
        send(n_send.at[dp * NZ], n_recv.at[i * NZ], ssem.at[3], rsem.at[3], (base + z, mp))

    @pl.when(mp == 1)
    def _():
        base = lax.rem(plane + NPLANE // 2, NPLANE) * NZ
        send(n_send.at[HALF], n_recv.at[0], ssem.at[4], rsem.at[4], (base + z, mp))

    @pl.when(mp == 0)
    def _():
        n_recv[0] = n_send[0]

    steps = ROWS // (2 * BLK)
    early = steps - 2

    @pl.loop(0, early // 2)
    def _(t):
        attend_pair(t)

    k_ch = k_c - mp * HALF
    slot_c = jnp.where((k_ch >= 0) & (k_ch < HALF), rank_c * HALF + k_ch, -1)
    k_rh = k_r - mp * HALF
    slot_r = jnp.where((k_rh >= 0) & (k_rh < HALF), rank_r * HALF + k_rh, -1)
    wait_bytes(n_recv.at[pl.ds(0, HALF - 1)], rsem.at[3])

    @pl.when(mp == 1)
    def _():
        wait_bytes(n_recv.at[0], rsem.at[4])

    fst[0 : HALF * 16, :] = n_recv[...].astype(F32).reshape(HALF * 16, 128)
    for j in range(CAP):
        for c in range(4):
            stack[j * HALF : (j + 1) * HALF, c * 128 : (c + 1) * 128] = fst[
                pl.ds(4 * j + c, HALF, stride=16), :
            ].astype(BF16)
    place_half = onehot(slot_c == iota((HR, CAP * HALF), 1))
    fn_send[...] = dot(place_half, stack[0 : CAP * HALF, :]).astype(BF16)
    send(fn_send, fn_recv, ssem.at[5], rsem.at[5], twin)

    @pl.loop(early // 2, steps // 2)
    def _(t):
        attend_pair(t)

    for part in range(4):
        apply(steps - 1, odd, part)

    dk_far = far_acc[:, 0:W].astype(BF16)
    dv_far = far_acc[:, W : 2 * W].astype(BF16)
    far_kv[...] = (dot(dk_far, wbuf[1], NT) + dot(dv_far, wbuf[2], NT)).astype(BF16)
    send(far_kv, t_recv, ssem.at[7], rsem.at[7], twin)
    wait_bytes(fn_recv, rsem.at[5])
    far_nodes = fn_send[...] + fn_recv[...]

    edge = 3 * W // 2
    for i in range(3):
        columns = slice(i * W, (i + 1) * W)
        part = jnp.zeros((2 * W, W), F32)
        for step in range(steps):
            part += dot(ntr[step], grads[step * 2 * BLK : (step + 1) * 2 * BLK, columns])
        if i == 1:
            part += dot(far_nodes, dk_far, TN)
        if i == 2:
            part += dot(far_nodes, dv_far, TN)
        gw[:, columns] = part
    a_send[...] = gw[:, 0:edge].astype(BF16).reshape(NY, 128, edge)
    for d in range(1, NY):
        yy = lax.rem(y + d, NY)
        send(a_send.at[yy], a_recv.at[d - 1], ssem.at[8], rsem.at[8], ((yy * NX + x) * NZ + z, mp))
    for yy in range(NY):
        for xx in range(NX):
            first = yy * 128 + xx * 32
            b_send[xx, yy] = gw[first : first + 32, edge:].astype(BF16)
    for d in range(1, NX):
        xx = lax.rem(x + d, NX)
        send(b_send.at[xx], b_recv.at[d - 1], ssem.at[14], rsem.at[14], ((y * NX + xx) * NZ + z, mp))

    place_t = onehot(slot_r == iota((CAP * HALF, HR), 0))
    wait_bytes(t_recv, rsem.at[7])
    summed = (far_kv[...].astype(F32) + t_recv[...].astype(F32)).astype(BF16)
    placed = dot(place_t, summed)
    for j in range(CAP):
        for c in range(4):
            fst[pl.ds(4 * j + c, HALF, stride=16), :] = placed[
                j * HALF : (j + 1) * HALF, c * 128 : (c + 1) * 128
            ]
    z_send[...] = fst[0 : HALF * 16, :].reshape(HALF, 16, 128).astype(BF16)

    @pl.loop(0, NPLANE // 2)
    def _(i):
        base = lax.rem(plane + first_plane + i, NPLANE) * NZ
        for dz in range(1, NZ):
            k = i * NZ + dz
            send(z_send.at[k], z_recv.at[k], ssem.at[9], rsem.at[9], (base + z_up[dz], mp))

    @pl.loop(1, NPLANE // 2)
    def _(i):
        base = lax.rem(plane + first_plane + i, NPLANE) * NZ
        send(z_send.at[i * NZ], z_recv.at[i * NZ], ssem.at[9], rsem.at[9], (base + z, mp))

    @pl.when(mp == 1)
    def _():
        base = lax.rem(plane + NPLANE // 2, NPLANE) * NZ
        send(z_send.at[0], z_recv.at[0], ssem.at[10], rsem.at[10], (base + z, mp))

    @pl.when(mp == 0)
    def _():
        z_recv[0] = z_send[0]

    @pl.loop(0, 4)
    def _(step):
        project(step)

    @pl.loop(4, steps)
    def _(step):
        project(step)

    wait_bytes(a_recv, rsem.at[8])
    own = gw[pl.ds(pl.multiple_of(y * 128, 128), 128), 0:edge]
    for d in range(NY - 1):
        own += a_recv[d].astype(F32)
    a_sum[...] = own
    a2_send[...] = own.astype(BF16).reshape(NX, 32, edge)
    for d in range(1, NX):
        xx = lax.rem(x + d, NX)
        send(a2_send.at[xx], a2_recv.at[d - 1], ssem.at[11], rsem.at[11], ((y * NX + xx) * NZ + z, mp))
    wait_bytes(b_recv, rsem.at[14])
    for yy in range(NY):
        own = gw[pl.ds(pl.multiple_of(yy * 128 + x * 32, 32), 32), edge:]
        for d in range(NX - 1):
            own += b_recv[d, yy].astype(F32)
        b_sum[yy * 32 : (yy + 1) * 32, :] = own
        b2_send[yy] = own.astype(BF16)
    for d in range(1, NY):
        yy = lax.rem(y + d, NY)
        send(b2_send.at[yy], b2_recv.at[d - 1], ssem.at[15], rsem.at[15], ((yy * NX + x) * NZ + z, mp))

    wait_bytes(a2_recv, rsem.at[11])
    wait_bytes(b2_recv, rsem.at[15])
    own_a = a_sum[pl.ds(pl.multiple_of(x * 32, 32), 32), :]
    own_b = b_sum[pl.ds(pl.multiple_of(y * 32, 32), 32), :]
    for d in range(NX - 1):
        own_a += a2_recv[d].astype(F32)
        own_b += b2_recv[d].astype(F32)
    for zz in range(NZ):
        for c in range(3):
            zz_send[zz, 4 * c : 4 * c + 4, :] = own_a[4 * zz : 4 * zz + 4, c * 128 : (c + 1) * 128]
            zz_send[zz, 4 * c + 12 : 4 * c + 16, :] = own_b[
                4 * zz : 4 * zz + 4, c * 128 : (c + 1) * 128
            ]
    for d in range(1, NZ):
        send(
            zz_send.at[z_up[d]], zz_recv.at[d], ssem.at[12], rsem.at[12], (plane * NZ + z_up[d], mp)
        )
    zz_recv[0] = zz_send[z]

    wait_bytes(z_recv.at[pl.ds(0, HALF - 1)], rsem.at[9])

    @pl.when(mp == 1)
    def _():
        wait_bytes(z_recv.at[0], rsem.at[10])

    fst[0 : HALF * 16, :] = z_recv[...].astype(F32).reshape(HALF * 16, 128)
    for j in range(CAP):
        for c in range(2):
            x_send[j, :, c * 128 : (c + 1) * 128] = fst[
                pl.ds(4 * j + 2 * (1 - mp) + c, HALF, stride=16), :
            ].astype(BF16)
    send(x_send, z_full.at[:, mp], ssem.at[13], rsem.at[13], twin)
    for j in range(CAP):
        for c in range(2):
            z_full[j, mp, :, c * 128 : (c + 1) * 128] = fst[
                pl.ds(4 * j + 2 * mp + c, HALF, stride=16), :
            ].astype(BF16)
    wait_bytes(e_recv, rsem.at[6])
    mine[...] += e_recv[...].astype(F32)

    wait_bytes(x_send, rsem.at[13])
    far = z_full[...].reshape(CAP * NG, W)

    @pl.loop(0, ROWS // 512)
    def _(i):
        rows = pl.ds(pl.multiple_of(i * 512, 512), 512)
        nodes_out[rows, :] = (mine[rows, :] + dot(scat[rows, :], far)).astype(BF16)

    wait_bytes(zz_recv.at[pl.ds(0, NZ - 1)], rsem.at[12])
    final = zz_recv[0]
    for d in range(1, NZ):
        final += zz_recv[d]
    for c in range(6):
        weights_out[c // 2, :, (c % 2) * 128 : (c % 2 + 1) * 128] = final[4 * c : 4 * c + 4, :]

    wait_bytes(s1.at[pl.ds(0, NZ - 1)], ssem.at[0])
    wait_bytes(r2.at[pl.ds(0, NPLANE - 1)], ssem.at[1])
    wait_bytes(kv_send.at[pl.ds(0, NG - 1)], ssem.at[2])
    wait_bytes(n_recv.at[pl.ds(0, HALF - 1)], ssem.at[3])
    wait_bytes(fn_recv, ssem.at[5])
    wait_bytes(e_recv, ssem.at[6])
    wait_bytes(t_recv, ssem.at[7])
    wait_bytes(a_recv, ssem.at[8])
    wait_bytes(b_recv, ssem.at[14])
    wait_bytes(z_recv.at[pl.ds(0, HALF - 1)], ssem.at[9])
    wait_bytes(a2_recv, ssem.at[11])
    wait_bytes(b2_recv, ssem.at[15])
    wait_bytes(zz_recv.at[pl.ds(0, NZ - 1)], ssem.at[12])
    wait_bytes(x_send, ssem.at[13])

    @pl.when(mp == 1)
    def _():
        wait_bytes(n_recv.at[0], ssem.at[4])
        wait_bytes(z_recv.at[0], ssem.at[10])


VM = pl.BlockSpec(memory_space=pltpu.VMEM)
HBM = pl.BlockSpec(memory_space=pltpu.HBM)
LIMIT = 56 * 1024 * 1024


def on_device(
    nodes_in, query, keys, values, grad_attn, w_query, w_key, w_value, halo_owner, halo_row, pattern
):
    dma = pltpu.SemaphoreType.DMA
    vm = pltpu.VMEM
    grad_nodes, grad_weights = pl.pallas_call(
        layer_kernel,
        out_shape=(
            jax.ShapeDtypeStruct((ROWS, W), BF16),
            jax.ShapeDtypeStruct((3, 4, W), F32),
        ),
        in_specs=[HBM] * 11,
        out_specs=(VM, VM),
        scratch_shapes=[
            vm((ROWS, W), BF16),
            vm((ROWS, W), BF16),
            vm((ROWS, W), BF16),
            vm((ROWS, W), BF16),
            vm((ROWS, 2 * W), BF16),
            vm((3, 2 * W, W), BF16),
            vm((NZ, 1, 128), I32),
            vm((NZ, 1, 128), I32),
            vm((8, 128), I32),
            vm((NPLANE, 8, 128), I32),
            vm((NG * 16, 128), F32),
            vm((NG, 16, 128), BF16),
            vm((NG, 16, 128), BF16),
            vm((NG, 16, 128), BF16),
            vm((HALF, 16, 128), BF16),
            vm((CAP * NG, 2 * W), BF16),
            vm((HR, 2 * W), BF16),
            vm((HR, 2 * W), BF16),
            pltpu.SMEM((2, ROWS // BLK), I32),
            vm((1, HR), I32),
            vm((1, HR), I32),
            vm((8, 128), I32),
            vm((HR, 2 * W), BF16),
            vm((W, HR), BF16),
            vm((HR, 2 * W), F32),
            vm((ROWS // 256, BLK, 8 * BLK), F32),
            vm((ROWS // 256, BLK, 8 * BLK), F32),
            vm((ROWS // 256, 8, 8 * BLK), F32),
            vm((2 * W, 3 * W), F32),
            vm((ROWS, W), F32),
            vm((ROWS, W), BF16),
            vm((ROWS // 256, 8 * BLK, W), BF16),
            vm((ROWS // 256, 8 * BLK, W), BF16),
            vm((ROWS // 256, W, 2 * BLK), BF16),
            vm((ROWS // 256, 2 * W, 2 * BLK), BF16),
            vm((ROWS, CAP * NG), BF16),
            vm((ROWS, 3 * W), BF16),
            vm((2, 3 * BLK, 8 * BLK), BF16),
            vm((2, 3 * BLK, 8 * BLK), BF16),
            vm((HR, 2 * W), BF16),
            vm((HALF, 16, 128), BF16),
            vm((HALF, 16, 128), BF16),
            vm((CAP, HALF, W), BF16),
            vm((CAP, 2, HALF, W), BF16),
            vm((NY, 128, 3 * W // 2), BF16),
            vm((NY - 1, 128, 3 * W // 2), BF16),
            vm((NX, NY, 32, 3 * W // 2), BF16),
            vm((NX - 1, NY, 32, 3 * W // 2), BF16),
            vm((128, 3 * W // 2), F32),
            vm((128, 3 * W // 2), F32),
            vm((NX, 32, 3 * W // 2), BF16),
            vm((NX - 1, 32, 3 * W // 2), BF16),
            vm((NY, 32, 3 * W // 2), BF16),
            vm((NY - 1, 32, 3 * W // 2), BF16),
            vm((NZ, 24, 128), F32),
            vm((NZ, 24, 128), F32),
            dma((11,)),
            dma((16,)),
            dma((20,)),
        ],
        compiler_params=pltpu.CompilerParams(
            collective_id=0, has_side_effects=True, vmem_limit_bytes=LIMIT
        ),
        name="layer",
    )(
        pattern.T, halo_owner.reshape(1, HR), halo_row.reshape(1, HR),
        query, keys, values, grad_attn, nodes_in, w_query, w_key, w_value,
    )
    return grad_nodes, jnp.transpose(grad_weights, (1, 0, 2))


def solution(mesh):
    in_specs = (
        P("graph", None),
        P("graph", "mp"),
        P("graph", "mp"),
        P("graph", "mp"),
        P("graph", "mp"),
        P(None, "mp"),
        P(None, "mp"),
        P(None, "mp"),
        P("graph", None),
        P("graph"),
        P("graph", None),
    )
    out_specs = (P("graph", "mp"), P("graph", None, "mp"))
    return jax.shard_map(
        on_device, mesh=mesh, in_specs=in_specs, out_specs=out_specs, check_vma=False
    )
```

```python
import functools
import math

import jax
import jax.numpy as jnp
from jax import lax
from jax.experimental import pallas as pl
from jax.experimental.pallas import tpu as pltpu
from jax.sharding import PartitionSpec as P

MESH = pl.DeviceIdType.MESH
F32 = jnp.float32
BF16 = jnp.bfloat16
I32 = jnp.int32

HEADS_LOCAL = 4
E = 64
BLK = 128
ROWS = 2048
W = 256
HR = 256
CAP = 4
NX, NY, NZ = 4, 4, 8
NG = NX * NY * NZ
NPLANE = NX * NY
HALF = NG // 2
LOG2E = 1.4426950408889634
NT = (((1,), (1,)), ((), ()))
TN = (((0,), (0,)), ((), ()))


def dot(a, b, dims=(((1,), (0,)), ((), ()))):
    return lax.dot_general(a, b, dims, preferred_element_type=F32)


def iota(shape, dim):
    return lax.broadcasted_iota(I32, shape, dim)


def place():
    me = lax.axis_index("graph")
    mp = lax.axis_index("mp")
    return me, mp, lax.div(me, NZ), lax.rem(me, NZ)


def peer(plane, z, dplane, dz):
    return lax.rem(plane + dplane, NPLANE) * NZ + lax.rem(z + dz, NZ)


def relative(owner, plane, z):
    dplane = ((owner >> 3) - plane + NPLANE) & (NPLANE - 1)
    dz = ((owner & 7) - z + NZ) & (NZ - 1)
    return dplane, dz


def rank_column(owner_c, owner_r):
    same = (owner_c == owner_r) & (iota((HR, HR), 1) < iota((HR, HR), 0))
    return jnp.sum(jnp.where(same, 1, 0), axis=1, keepdims=True)


def rank_row(owner_c, owner_r):
    same = (owner_c == owner_r) & (iota((HR, HR), 0) < iota((HR, HR), 1))
    return jnp.sum(jnp.where(same, 1, 0), axis=0, keepdims=True)


def onehot(mask):
    return jnp.where(mask, 1.0, 0.0).astype(BF16)


def wait_bytes(ref, sem):
    pltpu.make_async_copy(ref, ref, sem).wait()


def send(src, dst, ssem, rsem, dev):
    pltpu.make_async_remote_copy(
        src_ref=src, dst_ref=dst, send_sem=ssem, recv_sem=rsem, device_id=dev, device_id_type=MESH
    ).start()


def head_stack(x):
    head_of_lane = iota((2 * BLK, W), 1) // E
    return jnp.concatenate(
        [jnp.where(head_of_lane == h, x, 0.0).astype(BF16) for h in range(HEADS_LOCAL)], 0
    )


def block_rows(x, half):
    return jnp.concatenate(
        [x[(2 * h + half) * BLK : (2 * h + half + 1) * BLK, :] for h in range(HEADS_LOCAL)], 0
    )


def block_lanes(x, half):
    return jnp.concatenate(
        [x[:, (2 * h + half) * BLK : (2 * h + half + 1) * BLK] for h in range(HEADS_LOCAL)], 1
    )


def layer_kernel(
    pattern_hbm, owner_hbm, row_hbm,
    query_hbm, keys_hbm, values_hbm, grad_hbm, nodes_hbm, wq_hbm, wk_hbm, wv_hbm,
    nodes_out, weights_out,
    qbuf, kbuf, vbuf, gbuf, nbuf, wbuf,
    s1, r1, s2, r2, fst, kv_send, kv_recv, n_send, n_recv, stack, fn_send, fn_recv,
    pattern_ref, owner_ref, row_ref, asked_ref, far_kv, far_kt, far_acc, pbuf, dbuf, stats, gw, mine, e_recv,
    qms, gms, kts, ntr, scat, grads, even, odd,
    t_recv, z_send, z_recv, x_send, z_full,
    a_send, a_recv, b_send, b_recv, a_sum, b_sum, a2_send, a2_recv, b2_send, b2_recv,
    zz_send, zz_recv,
    lsem, ssem, rsem,
):
    me, mp, plane, z = place()
    y, x = lax.div(plane, NX), lax.rem(plane, NX)
    twin = (me, 1 - mp)
    loads = [
        pltpu.make_async_copy(src, dst, lsem.at[i])
        for i, (src, dst) in enumerate(
            (
                (keys_hbm, kbuf),
                (values_hbm, vbuf),
                (query_hbm, qbuf),
                (grad_hbm, gbuf),
                (nodes_hbm, nbuf),
                (wq_hbm, wbuf.at[0]),
                (wk_hbm, wbuf.at[1]),
                (wv_hbm, wbuf.at[2]),
                (owner_hbm, owner_ref),
                (row_hbm, row_ref),
                (pattern_hbm, pattern_ref),
            )
        )
    ]
    z_up = [lax.rem(z + d, NZ) for d in range(NZ)]
    z_down = [lax.rem(z - d + NZ, NZ) for d in range(NZ)]

    barrier = pltpu.get_barrier_semaphore()
    for d in range(1, NZ):
        pl.semaphore_signal(barrier, inc=1, device_id=(plane * NZ + z_up[d], mp), device_id_type=MESH)
    for d in range(1, NPLANE):
        pl.semaphore_signal(barrier, inc=1, device_id=(peer(plane, z, d, 0), mp), device_id_type=MESH)
    pl.semaphore_signal(barrier, inc=1, device_id=twin, device_id_type=MESH)

    for load in loads[8:] + loads[0:2]:
        load.start()

    for load in loads[8:]:
        load.wait()
    owner_r, row_r = owner_ref[...], row_ref[...]
    owner_c = jnp.broadcast_to(owner_r, (HR, HR)).T
    rank_c = rank_column(owner_c, owner_r)
    rank_r = rank_row(owner_c, owner_r)
    dplane_c, dz_c = relative(owner_c[:, 0:1], plane, z)
    dplane_r, dz_r = relative(owner_r, plane, z)
    column = onehot(dplane_c * CAP + rank_c == iota((HR, 128), 1))
    value = row_r + 1
    at_z = dz_r == iota((NZ, HR), 0)
    high = jnp.where(at_z, value >> 6, 0).astype(F32).astype(BF16)
    low = jnp.where(at_z, value & 63, 0).astype(F32).astype(BF16)
    wanted = (dot(high, column) * 64.0 + dot(low, column)).astype(I32) - 1
    for dz in range(NZ):
        s1[dz] = wanted[dz : dz + 1, :]
    k_c = dplane_c * NZ + dz_c
    k_r = dplane_r * NZ + dz_r
    pl.semaphore_wait(barrier, NZ - 1 + NPLANE - 1 + 1)

    for dz in range(1, NZ):
        send(s1.at[dz], r1.at[dz], ssem.at[0], rsem.at[0], (plane * NZ + z_up[dz], mp))
    r1[0] = s1[0]
    wait_bytes(r1.at[pl.ds(0, NZ - 1)], rsem.at[0])
    sub = iota((8, 128), 0)
    gathered = jnp.zeros((8, 128), I32)
    for dz in range(NZ):
        gathered = jnp.where(sub == dz, r1[dz], gathered)
    s2[...] = gathered
    for dp in range(1, NPLANE):
        send(s2, r2.at[dp], ssem.at[1], rsem.at[1], (peer(plane, z, dp, 0), mp))
    r2[0] = gathered
    wait_bytes(r2.at[pl.ds(0, NPLANE - 1)], rsem.at[1])

    for load in loads[2:8]:
        load.start()
    table = r2[...].reshape(NG, 128)
    table_t = table.T
    lanes, subs = iota((NG, 128), 1), iota((NG, 128), 0)
    asked = []
    for j in range(CAP):
        asked.append(
            jnp.sum(jnp.where(lanes == (subs >> 3) * CAP + j, table, 0), axis=1, keepdims=True)
        )
        asked_ref[j : j + 1, :] = jnp.sum(
            jnp.where(subs == (lanes >> 3) * CAP + j, table_t, 0), axis=0, keepdims=True
        )

    loads[0].wait()
    loads[1].wait()
    for part in range(2):
        ks = slice(part * HALF, (part + 1) * HALF)
        pick = jnp.concatenate(
            [onehot(asked[j][ks] == iota((HALF, ROWS), 1)) for j in range(CAP)], 0
        )
        part_k = dot(pick, kbuf[...])
        part_v = dot(pick, vbuf[...])
        for j in range(CAP):
            rows = slice(j * HALF, (j + 1) * HALF)
            first = part * HALF * 16 + 4 * j
            for c in range(2):
                cols = slice(c * 128, (c + 1) * 128)
                fst[pl.ds(first + c, HALF, stride=16), :] = part_k[rows, cols]
                fst[pl.ds(first + 2 + c, HALF, stride=16), :] = part_v[rows, cols]
        kv_send[ks] = (
            fst[part * HALF * 16 : (part + 1) * HALF * 16, :].reshape(HALF, 16, 128).astype(BF16)
        )

        @pl.loop(part * NPLANE // 2, (part + 1) * NPLANE // 2)
        def _(dp):
            base = lax.rem(plane - dp + NPLANE, NPLANE) * NZ
            for dz in (4, 3, 5, 2, 6, 1, 7):
                k = dp * NZ + dz
                send(kv_send.at[k], kv_recv.at[k], ssem.at[2], rsem.at[2], (base + z_down[dz], mp))

    @pl.loop(1, NPLANE)
    def _(dp):
        base = lax.rem(plane - dp + NPLANE, NPLANE) * NZ
        send(kv_send.at[dp * NZ], kv_recv.at[dp * NZ], ssem.at[2], rsem.at[2], (base + z, mp))

    kv_recv[0] = kv_send[0]

    for load in loads[2:8]:
        load.wait()

    @pl.loop(0, ROWS // (2 * BLK))
    def _(step):
        both = pl.ds(pl.multiple_of(step * 2 * BLK, 2 * BLK), 2 * BLK)
        qm = head_stack(qbuf[both, :] * 0.125)
        gm = head_stack(gbuf[both, :])
        qms[step] = qm
        gms[step] = gm
        kts[step] = (kbuf[both, :] * 0.125).T
        ntr[step] = nbuf[both, :].T
        for half in range(2):
            rows = pl.ds(pl.multiple_of(step * 2 * BLK + half * BLK, BLK), BLK)
            s_own = dot(kbuf[rows, :], block_rows(qm, half), NT)
            d_own = dot(vbuf[rows, :], block_rows(gm, half), NT)
            top = jnp.max(s_own, 0, keepdims=True)
            p_own = jnp.exp2((s_own - top) * LOG2E)
            total = jnp.sum(p_own, 0, keepdims=True)
            term = jnp.sum(p_own * d_own, 0, keepdims=True)
            for h in range(HEADS_LOCAL):
                src = slice(h * BLK, (h + 1) * BLK)
                dst = slice((2 * h + half) * BLK, (2 * h + half + 1) * BLK)
                pbuf[step, :, dst] = p_own[:, src]
                dbuf[step, :, dst] = d_own[:, src]
                stats[step, 0:1, dst] = top[:, src]
                stats[step, 1:2, dst] = total[:, src]
                stats[step, 2:3, dst] = term[:, src]

    for j in range(CAP):
        pick = onehot(asked[j] == iota((NG, ROWS), 1))
        part_n = dot(pick, nbuf[...])
        for c in range(4):
            fst[pl.ds(4 * j + c, NG, stride=16), :] = part_n[:, c * 128 : (c + 1) * 128]
    n_send[...] = fst[...].reshape(NG, 16, 128).astype(BF16)
    far_acc[...] = jnp.zeros_like(far_acc)
    odd[...] = jnp.zeros_like(odd)

    @pl.loop(0, ROWS // 256)
    def _(i):
        base = pl.multiple_of(i * 256, 256)
        row = iota((256, NG), 0) + base
        for j in range(CAP):
            scat[pl.ds(base, 256), j * NG : (j + 1) * NG] = onehot(row == asked_ref[j : j + 1, :])


    wait_bytes(kv_recv.at[pl.ds(0, NG - 1)], rsem.at[2])
    fst[...] = kv_recv[...].astype(F32).reshape(NG * 16, 128)
    for j in range(CAP):
        for c in range(4):
            stack[j * NG : (j + 1) * NG, c * 128 : (c + 1) * 128] = fst[
                pl.ds(4 * j + c, NG, stride=16), :
            ].astype(BF16)
    place_mat = onehot(rank_c * NG + k_c == iota((HR, CAP * NG), 1))
    far_kv[...] = dot(place_mat, stack[...]).astype(BF16)
    far_kt[...] = (far_kv[:, 0:W] * 0.125).T

    mine_rows = pl.ds(pl.multiple_of(mp * W, W), W)
    other_rows = pl.ds(pl.multiple_of((1 - mp) * W, W), W)

    def scores(step, h):
        rows = slice(2 * h * BLK, 2 * (h + 1) * BLK)
        first = h // 2 * 128
        pair = slice(first, first + 128)
        return (
            dot(far_kv[:, pair], qms[step, rows, pair], NT),
            dot(far_kv[:, W + first : W + first + 128], gms[step, rows, pair], NT),
        )

    def soften(step, h, bias, s_far, d_far, buf):
        lanes = slice(2 * h * BLK, 2 * (h + 1) * BLK)
        top_own = stats[step, 0:1, lanes]
        top = jnp.maximum(
            top_own,
            jnp.maximum(
                jnp.max(s_far[0:BLK], 0, keepdims=True) - bias[0],
                jnp.max(s_far[BLK:], 0, keepdims=True) - bias[1],
            ),
        )
        p_far = jnp.concatenate(
            [
                jnp.exp2((s_far[0:BLK] - (top + bias[0])) * LOG2E),
                jnp.exp2((s_far[BLK:] - (top + bias[1])) * LOG2E),
            ],
            0,
        )
        share = jnp.exp2((top_own - top) * LOG2E)
        inv = 1.0 / (stats[step, 1:2, lanes] * share + jnp.sum(p_far, 0, keepdims=True))
        term = (stats[step, 2:3, lanes] * share + jnp.sum(p_far * d_far, 0, keepdims=True)) * inv
        prob_own = pbuf[step, :, lanes] * (share * inv)
        prob_far = p_far * inv
        buf[0, 0:BLK, lanes] = (prob_own * (dbuf[step, :, lanes] - term)).astype(BF16)
        buf[0, BLK:, lanes] = (prob_far * (d_far - term)).astype(BF16)
        buf[1, 0:BLK, lanes] = prob_own.astype(BF16)
        buf[1, BLK:, lanes] = prob_far.astype(BF16)

    def apply(step, buf, part):
        first = pl.multiple_of(step * 2 * BLK, 2 * BLK)
        if part < 2:
            stacked = (qms, gms)[part]
            for pair in range(2):
                span = slice(pair * 4 * BLK, (pair + 1) * 4 * BLK)
                lane = part * W + pair * 128
                far_acc[:, lane : lane + 128] += dot(
                    buf[part, BLK:, span], stacked[step, span, pair * 128 : (pair + 1) * 128]
                )
        elif part == 2:
            pieces = []
            for h in range(HEADS_LOCAL):
                heads = slice(h * E, (h + 1) * E)
                own_part = [
                    dot(
                        kts[step, heads, half * BLK : (half + 1) * BLK],
                        buf[0, 0:BLK, (2 * h + half) * BLK : (2 * h + half + 1) * BLK],
                    )
                    for half in range(2)
                ]
                pieces.append(
                    dot(far_kt[heads, :], buf[0, BLK:, 2 * h * BLK : 2 * (h + 1) * BLK])
                    + jnp.concatenate(own_part, 1)
                )
            grads[pl.ds(first, 2 * BLK), 0:W] = jnp.concatenate(pieces, 0).T.astype(BF16)
        else:
            for i, stacked in enumerate((qms, gms)):
                for half in range(2):
                    rows = pl.ds(pl.multiple_of(first + half * BLK, BLK), BLK)
                    grads[rows, (i + 1) * W : (i + 2) * W] = dot(
                        block_lanes(buf[i, 0:BLK, :], half), block_rows(stacked[step], half)
                    ).astype(BF16)

    def attend(step, buf, before, buf_before):
        second = ((iota((1, 2 * BLK), 1) >> 7) & 1) == 1
        bias = []
        for h in range(2):
            each = [
                jnp.where(pattern_ref[h, 2 * step + half] > 0, 0.0, 1e30).astype(F32)
                for half in range(2)
            ]
            bias.append(jnp.where(second, each[1], each[0]))
        ready = scores(step, 0)
        for h in range(HEADS_LOCAL):
            now = ready
            if h + 1 < HEADS_LOCAL:
                ready = scores(step, h + 1)
            apply(before, buf_before, h)
            soften(step, h, bias, now[0], now[1], buf)

    def attend_pair(t):
        attend(2 * t, even, jnp.maximum(2 * t - 1, 0), odd)
        attend(2 * t + 1, odd, 2 * t, even)

    def project(step):
        both = pl.ds(pl.multiple_of(step * 2 * BLK, 2 * BLK), 2 * BLK)
        kept = jnp.zeros((2 * BLK, W), F32)
        given = jnp.zeros((2 * BLK, W), F32)
        for i in range(3):
            grad = grads[both, i * W : (i + 1) * W]
            kept += dot(grad, wbuf[i, mine_rows, :], NT)
            given += dot(grad, wbuf[i, other_rows, :], NT)
        mine[both, :] = kept
        gbuf[both, :] = given.astype(BF16)
        send(gbuf.at[both], e_recv.at[both], ssem.at[6], rsem.at[6], twin)

    first_plane = mp * (NPLANE // 2)

    @pl.loop(0, NPLANE // 2)
    def _(i):
        dp = first_plane + i
        base = lax.rem(plane - dp + NPLANE, NPLANE) * NZ
        for dz in range(1, NZ):
            send(
                n_send.at[dp * NZ + dz], n_recv.at[i * NZ + dz], ssem.at[3], rsem.at[3],
                (base + z_down[dz], mp),
            )

    @pl.loop(1, NPLANE // 2)
    def _(i):
        dp = first_plane + i
        base = lax.rem(plane - dp + NPLANE, NPLANE) * NZ
        send(n_send.at[dp * NZ], n_recv.at[i * NZ], ssem.at[3], rsem.at[3], (base + z, mp))

    @pl.when(mp == 1)
    def _():
        base = lax.rem(plane + NPLANE // 2, NPLANE) * NZ
        send(n_send.at[HALF], n_recv.at[0], ssem.at[4], rsem.at[4], (base + z, mp))

    @pl.when(mp == 0)
    def _():
        n_recv[0] = n_send[0]

    steps = ROWS // (2 * BLK)
    early = steps - 2

    @pl.loop(0, early // 2)
    def _(t):
        attend_pair(t)

    k_ch = k_c - mp * HALF
    slot_c = jnp.where((k_ch >= 0) & (k_ch < HALF), rank_c * HALF + k_ch, -1)
    k_rh = k_r - mp * HALF
    slot_r = jnp.where((k_rh >= 0) & (k_rh < HALF), rank_r * HALF + k_rh, -1)
    wait_bytes(n_recv.at[pl.ds(0, HALF - 1)], rsem.at[3])

    @pl.when(mp == 1)
    def _():
        wait_bytes(n_recv.at[0], rsem.at[4])

    fst[0 : HALF * 16, :] = n_recv[...].astype(F32).reshape(HALF * 16, 128)
    for j in range(CAP):
        for c in range(4):
            stack[j * HALF : (j + 1) * HALF, c * 128 : (c + 1) * 128] = fst[
                pl.ds(4 * j + c, HALF, stride=16), :
            ].astype(BF16)
    place_half = onehot(slot_c == iota((HR, CAP * HALF), 1))
    fn_send[...] = dot(place_half, stack[0 : CAP * HALF, :]).astype(BF16)
    send(fn_send, fn_recv, ssem.at[5], rsem.at[5], twin)

    @pl.loop(early // 2, steps // 2)
    def _(t):
        attend_pair(t)

    for part in range(4):
        apply(steps - 1, odd, part)

    dk_far = far_acc[:, 0:W].astype(BF16)
    dv_far = far_acc[:, W : 2 * W].astype(BF16)
    far_kv[...] = (dot(dk_far, wbuf[1], NT) + dot(dv_far, wbuf[2], NT)).astype(BF16)
    send(far_kv, t_recv, ssem.at[7], rsem.at[7], twin)
    wait_bytes(fn_recv, rsem.at[5])
    far_nodes = fn_send[...] + fn_recv[...]

    edge = 3 * W // 2
    for i in range(3):
        columns = slice(i * W, (i + 1) * W)
        part = jnp.zeros((2 * W, W), F32)
        for step in range(steps):
            part += dot(ntr[step], grads[step * 2 * BLK : (step + 1) * 2 * BLK, columns])
        if i == 1:
            part += dot(far_nodes, dk_far, TN)
        if i == 2:
            part += dot(far_nodes, dv_far, TN)
        gw[:, columns] = part
    a_send[...] = gw[:, 0:edge].astype(BF16).reshape(NY, 128, edge)
    for d in range(1, NY):
        yy = lax.rem(y + d, NY)
        send(a_send.at[yy], a_recv.at[d - 1], ssem.at[8], rsem.at[8], ((yy * NX + x) * NZ + z, mp))
    for yy in range(NY):
        for xx in range(NX):
            first = yy * 128 + xx * 32
            b_send[xx, yy] = gw[first : first + 32, edge:].astype(BF16)
    for d in range(1, NX):
        xx = lax.rem(x + d, NX)
        send(b_send.at[xx], b_recv.at[d - 1], ssem.at[14], rsem.at[14], ((y * NX + xx) * NZ + z, mp))

    place_t = onehot(slot_r == iota((CAP * HALF, HR), 0))
    wait_bytes(t_recv, rsem.at[7])
    summed = (far_kv[...].astype(F32) + t_recv[...].astype(F32)).astype(BF16)
    placed = dot(place_t, summed)
    for j in range(CAP):
        for c in range(4):
            fst[pl.ds(4 * j + c, HALF, stride=16), :] = placed[
                j * HALF : (j + 1) * HALF, c * 128 : (c + 1) * 128
            ]
    z_send[...] = fst[0 : HALF * 16, :].reshape(HALF, 16, 128).astype(BF16)

    @pl.loop(0, NPLANE // 2)
    def _(i):
        base = lax.rem(plane + first_plane + i, NPLANE) * NZ
        for dz in range(1, NZ):
            k = i * NZ + dz
            send(z_send.at[k], z_recv.at[k], ssem.at[9], rsem.at[9], (base + z_up[dz], mp))

    @pl.loop(1, NPLANE // 2)
    def _(i):
        base = lax.rem(plane + first_plane + i, NPLANE) * NZ
        send(z_send.at[i * NZ], z_recv.at[i * NZ], ssem.at[9], rsem.at[9], (base + z, mp))

    @pl.when(mp == 1)
    def _():
        base = lax.rem(plane + NPLANE // 2, NPLANE) * NZ
        send(z_send.at[0], z_recv.at[0], ssem.at[10], rsem.at[10], (base + z, mp))

    @pl.when(mp == 0)
    def _():
        z_recv[0] = z_send[0]

    @pl.loop(0, 4)
    def _(step):
        project(step)

    @pl.loop(4, steps)
    def _(step):
        project(step)

    wait_bytes(a_recv, rsem.at[8])
    own = gw[pl.ds(pl.multiple_of(y * 128, 128), 128), 0:edge]
    for d in range(NY - 1):
        own += a_recv[d].astype(F32)
    a_sum[...] = own
    a2_send[...] = own.astype(BF16).reshape(NX, 32, edge)
    for d in range(1, NX):
        xx = lax.rem(x + d, NX)
        send(a2_send.at[xx], a2_recv.at[d - 1], ssem.at[11], rsem.at[11], ((y * NX + xx) * NZ + z, mp))
    wait_bytes(b_recv, rsem.at[14])
    for yy in range(NY):
        own = gw[pl.ds(pl.multiple_of(yy * 128 + x * 32, 32), 32), edge:]
        for d in range(NX - 1):
            own += b_recv[d, yy].astype(F32)
        b_sum[yy * 32 : (yy + 1) * 32, :] = own
        b2_send[yy] = own.astype(BF16)
    for d in range(1, NY):
        yy = lax.rem(y + d, NY)
        send(b2_send.at[yy], b2_recv.at[d - 1], ssem.at[15], rsem.at[15], ((yy * NX + x) * NZ + z, mp))

    wait_bytes(a2_recv, rsem.at[11])
    wait_bytes(b2_recv, rsem.at[15])
    own_a = a_sum[pl.ds(pl.multiple_of(x * 32, 32), 32), :]
    own_b = b_sum[pl.ds(pl.multiple_of(y * 32, 32), 32), :]
    for d in range(NX - 1):
        own_a += a2_recv[d].astype(F32)
        own_b += b2_recv[d].astype(F32)
    for zz in range(NZ):
        for c in range(3):
            zz_send[zz, 4 * c : 4 * c + 4, :] = own_a[4 * zz : 4 * zz + 4, c * 128 : (c + 1) * 128]
            zz_send[zz, 4 * c + 12 : 4 * c + 16, :] = own_b[
                4 * zz : 4 * zz + 4, c * 128 : (c + 1) * 128
            ]
    for d in range(1, NZ):
        send(
            zz_send.at[z_up[d]], zz_recv.at[d], ssem.at[12], rsem.at[12], (plane * NZ + z_up[d], mp)
        )
    zz_recv[0] = zz_send[z]

    wait_bytes(z_recv.at[pl.ds(0, HALF - 1)], rsem.at[9])

    @pl.when(mp == 1)
    def _():
        wait_bytes(z_recv.at[0], rsem.at[10])

    fst[0 : HALF * 16, :] = z_recv[...].astype(F32).reshape(HALF * 16, 128)
    for j in range(CAP):
        for c in range(2):
            x_send[j, :, c * 128 : (c + 1) * 128] = fst[
                pl.ds(4 * j + 2 * (1 - mp) + c, HALF, stride=16), :
            ].astype(BF16)
    send(x_send, z_full.at[:, mp], ssem.at[13], rsem.at[13], twin)
    for j in range(CAP):
        for c in range(2):
            z_full[j, mp, :, c * 128 : (c + 1) * 128] = fst[
                pl.ds(4 * j + 2 * mp + c, HALF, stride=16), :
            ].astype(BF16)
    wait_bytes(e_recv, rsem.at[6])
    mine[...] += e_recv[...].astype(F32)

    wait_bytes(x_send, rsem.at[13])
    far = z_full[...].reshape(CAP * NG, W)

    @pl.loop(0, ROWS // 512)
    def _(i):
        rows = pl.ds(pl.multiple_of(i * 512, 512), 512)
        nodes_out[rows, :] = (mine[rows, :] + dot(scat[rows, :], far)).astype(BF16)

    wait_bytes(zz_recv.at[pl.ds(0, NZ - 1)], rsem.at[12])
    final = zz_recv[0]
    for d in range(1, NZ):
        final += zz_recv[d]
    for c in range(6):
        weights_out[c // 2, :, (c % 2) * 128 : (c % 2 + 1) * 128] = final[4 * c : 4 * c + 4, :]

    wait_bytes(s1.at[pl.ds(0, NZ - 1)], ssem.at[0])
    wait_bytes(r2.at[pl.ds(0, NPLANE - 1)], ssem.at[1])
    wait_bytes(kv_send.at[pl.ds(0, NG - 1)], ssem.at[2])
    wait_bytes(n_recv.at[pl.ds(0, HALF - 1)], ssem.at[3])
    wait_bytes(fn_recv, ssem.at[5])
    wait_bytes(e_recv, ssem.at[6])
    wait_bytes(t_recv, ssem.at[7])
    wait_bytes(a_recv, ssem.at[8])
    wait_bytes(b_recv, ssem.at[14])
    wait_bytes(z_recv.at[pl.ds(0, HALF - 1)], ssem.at[9])
    wait_bytes(a2_recv, ssem.at[11])
    wait_bytes(b2_recv, ssem.at[15])
    wait_bytes(zz_recv.at[pl.ds(0, NZ - 1)], ssem.at[12])
    wait_bytes(x_send, ssem.at[13])

    @pl.when(mp == 1)
    def _():
        wait_bytes(n_recv.at[0], ssem.at[4])
        wait_bytes(z_recv.at[0], ssem.at[10])


VM = pl.BlockSpec(memory_space=pltpu.VMEM)
HBM = pl.BlockSpec(memory_space=pltpu.HBM)
LIMIT = 56 * 1024 * 1024


def on_device(
    nodes_in, query, keys, values, grad_attn, w_query, w_key, w_value, halo_owner, halo_row, pattern
):
    dma = pltpu.SemaphoreType.DMA
    vm = pltpu.VMEM
    grad_nodes, grad_weights = pl.pallas_call(
        layer_kernel,
        out_shape=(
            jax.ShapeDtypeStruct((ROWS, W), BF16),
            jax.ShapeDtypeStruct((3, 4, W), F32),
        ),
        in_specs=[HBM] * 11,
        out_specs=(VM, VM),
        scratch_shapes=[
            vm((ROWS, W), BF16),
            vm((ROWS, W), BF16),
            vm((ROWS, W), BF16),
            vm((ROWS, W), BF16),
            vm((ROWS, 2 * W), BF16),
            vm((3, 2 * W, W), BF16),
            vm((NZ, 1, 128), I32),
            vm((NZ, 1, 128), I32),
            vm((8, 128), I32),
            vm((NPLANE, 8, 128), I32),
            vm((NG * 16, 128), F32),
            vm((NG, 16, 128), BF16),
            vm((NG, 16, 128), BF16),
            vm((NG, 16, 128), BF16),
            vm((HALF, 16, 128), BF16),
            vm((CAP * NG, 2 * W), BF16),
            vm((HR, 2 * W), BF16),
            vm((HR, 2 * W), BF16),
            pltpu.SMEM((2, ROWS // BLK), I32),
            vm((1, HR), I32),
            vm((1, HR), I32),
            vm((8, 128), I32),
            vm((HR, 2 * W), BF16),
            vm((W, HR), BF16),
            vm((HR, 2 * W), F32),
            vm((ROWS // 256, BLK, 8 * BLK), F32),
            vm((ROWS // 256, BLK, 8 * BLK), F32),
            vm((ROWS // 256, 8, 8 * BLK), F32),
            vm((2 * W, 3 * W), F32),
            vm((ROWS, W), F32),
            vm((ROWS, W), BF16),
            vm((ROWS // 256, 8 * BLK, W), BF16),
            vm((ROWS // 256, 8 * BLK, W), BF16),
            vm((ROWS // 256, W, 2 * BLK), BF16),
            vm((ROWS // 256, 2 * W, 2 * BLK), BF16),
            vm((ROWS, CAP * NG), BF16),
            vm((ROWS, 3 * W), BF16),
            vm((2, 3 * BLK, 8 * BLK), BF16),
            vm((2, 3 * BLK, 8 * BLK), BF16),
            vm((HR, 2 * W), BF16),
            vm((HALF, 16, 128), BF16),
            vm((HALF, 16, 128), BF16),
            vm((CAP, HALF, W), BF16),
            vm((CAP, 2, HALF, W), BF16),
            vm((NY, 128, 3 * W // 2), BF16),
            vm((NY - 1, 128, 3 * W // 2), BF16),
            vm((NX, NY, 32, 3 * W // 2), BF16),
            vm((NX - 1, NY, 32, 3 * W // 2), BF16),
            vm((128, 3 * W // 2), F32),
            vm((128, 3 * W // 2), F32),
            vm((NX, 32, 3 * W // 2), BF16),
            vm((NX - 1, 32, 3 * W // 2), BF16),
            vm((NY, 32, 3 * W // 2), BF16),
            vm((NY - 1, 32, 3 * W // 2), BF16),
            vm((NZ, 24, 128), F32),
            vm((NZ, 24, 128), F32),
            dma((11,)),
            dma((16,)),
            dma((20,)),
        ],
        compiler_params=pltpu.CompilerParams(
            collective_id=0, has_side_effects=True, vmem_limit_bytes=LIMIT
        ),
        name="layer",
    )(
        pattern.T, halo_owner.reshape(1, HR), halo_row.reshape(1, HR),
        query, keys, values, grad_attn, nodes_in, w_query, w_key, w_value,
    )
    return grad_nodes, jnp.transpose(grad_weights, (1, 0, 2))


def solution(mesh):
    in_specs = (
        P("graph", None),
        P("graph", "mp"),
        P("graph", "mp"),
        P("graph", "mp"),
        P("graph", "mp"),
        P(None, "mp"),
        P(None, "mp"),
        P(None, "mp"),
        P("graph", None),
        P("graph"),
        P("graph", None),
    )
    out_specs = (P("graph", "mp"), P("graph", None, "mp"))
    return jax.shard_map(
        on_device, mesh=mesh, in_specs=in_specs, out_specs=out_specs, check_vma=False
    )
```

```python
import functools
import math

import jax
import jax.numpy as jnp
from jax import lax
from jax.experimental import pallas as pl
from jax.experimental.pallas import tpu as pltpu
from jax.sharding import PartitionSpec as P

MESH = pl.DeviceIdType.MESH
F32 = jnp.float32
BF16 = jnp.bfloat16
I32 = jnp.int32

HEADS_LOCAL = 4
E = 64
BLK = 128
ROWS = 2048
W = 256
HR = 256
CAP = 4
NX, NY, NZ = 4, 4, 8
NG = NX * NY * NZ
NPLANE = NX * NY
HALF = NG // 2
LOG2E = 1.4426950408889634
NT = (((1,), (1,)), ((), ()))
TN = (((0,), (0,)), ((), ()))


def dot(a, b, dims=(((1,), (0,)), ((), ()))):
    return lax.dot_general(a, b, dims, preferred_element_type=F32)


def iota(shape, dim):
    return lax.broadcasted_iota(I32, shape, dim)


def place():
    me = lax.axis_index("graph")
    mp = lax.axis_index("mp")
    return me, mp, lax.div(me, NZ), lax.rem(me, NZ)


def peer(plane, z, dplane, dz):
    return lax.rem(plane + dplane, NPLANE) * NZ + lax.rem(z + dz, NZ)


def relative(owner, plane, z):
    dplane = ((owner >> 3) - plane + NPLANE) & (NPLANE - 1)
    dz = ((owner & 7) - z + NZ) & (NZ - 1)
    return dplane, dz


def rank_column(owner_c, owner_r):
    same = (owner_c == owner_r) & (iota((HR, HR), 1) < iota((HR, HR), 0))
    return jnp.sum(jnp.where(same, 1, 0), axis=1, keepdims=True)


def rank_row(owner_c, owner_r):
    same = (owner_c == owner_r) & (iota((HR, HR), 0) < iota((HR, HR), 1))
    return jnp.sum(jnp.where(same, 1, 0), axis=0, keepdims=True)


def onehot(mask):
    return jnp.where(mask, 1.0, 0.0).astype(BF16)


def wait_bytes(ref, sem):
    pltpu.make_async_copy(ref, ref, sem).wait()


def send(src, dst, ssem, rsem, dev):
    pltpu.make_async_remote_copy(
        src_ref=src, dst_ref=dst, send_sem=ssem, recv_sem=rsem, device_id=dev, device_id_type=MESH
    ).start()


def head_stack(x):
    head_of_lane = iota((2 * BLK, W), 1) // E
    return jnp.concatenate(
        [jnp.where(head_of_lane == h, x, 0.0).astype(BF16) for h in range(HEADS_LOCAL)], 0
    )


def block_rows(x, half):
    return jnp.concatenate(
        [x[(2 * h + half) * BLK : (2 * h + half + 1) * BLK, :] for h in range(HEADS_LOCAL)], 0
    )


def block_lanes(x, half):
    return jnp.concatenate(
        [x[:, (2 * h + half) * BLK : (2 * h + half + 1) * BLK] for h in range(HEADS_LOCAL)], 1
    )


def layer_kernel(
    pattern_hbm, owner_hbm, row_hbm,
    query_hbm, keys_hbm, values_hbm, grad_hbm, nodes_hbm, wq_hbm, wk_hbm, wv_hbm,
    nodes_out, weights_out,
    qbuf, kbuf, vbuf, gbuf, nbuf, wbuf,
    s1, r1, s2, r2, fst, kv_send, kv_recv, n_send, n_recv, stack, fn_send, fn_recv,
    pattern_ref, owner_ref, row_ref, asked_ref, far_kv, far_kt, far_acc, pbuf, dbuf, stats, gw, mine, e_recv,
    qms, gms, kts, ntr, scat, grads, even, odd,
    t_recv, z_send, z_recv, x_send, z_full,
    a_send, a_recv, b_send, b_recv, a_sum, b_sum, a2_send, a2_recv, b2_send, b2_recv,
    zz_send, zz_recv,
    lsem, ssem, rsem,
):
    me, mp, plane, z = place()
    y, x = lax.div(plane, NX), lax.rem(plane, NX)
    twin = (me, 1 - mp)
    loads = [
        pltpu.make_async_copy(src, dst, lsem.at[i])
        for i, (src, dst) in enumerate(
            (
                (keys_hbm, kbuf),
                (values_hbm, vbuf),
                (query_hbm, qbuf),
                (grad_hbm, gbuf),
                (nodes_hbm, nbuf),
                (wq_hbm, wbuf.at[0]),
                (wk_hbm, wbuf.at[1]),
                (wv_hbm, wbuf.at[2]),
                (owner_hbm, owner_ref),
                (row_hbm, row_ref),
                (pattern_hbm, pattern_ref),
            )
        )
    ]
    z_up = [lax.rem(z + d, NZ) for d in range(NZ)]
    z_down = [lax.rem(z - d + NZ, NZ) for d in range(NZ)]

    barrier = pltpu.get_barrier_semaphore()
    for d in range(1, NZ):
        pl.semaphore_signal(barrier, inc=1, device_id=(plane * NZ + z_up[d], mp), device_id_type=MESH)
    for d in range(1, NPLANE):
        pl.semaphore_signal(barrier, inc=1, device_id=(peer(plane, z, d, 0), mp), device_id_type=MESH)
    pl.semaphore_signal(barrier, inc=1, device_id=twin, device_id_type=MESH)

    for load in loads[8:] + loads[0:2]:
        load.start()

    for load in loads[8:]:
        load.wait()
    owner_r, row_r = owner_ref[...], row_ref[...]
    owner_c = jnp.broadcast_to(owner_r, (HR, HR)).T
    rank_c = rank_column(owner_c, owner_r)
    rank_r = rank_row(owner_c, owner_r)
    dplane_c, dz_c = relative(owner_c[:, 0:1], plane, z)
    dplane_r, dz_r = relative(owner_r, plane, z)
    column = onehot(dplane_c * CAP + rank_c == iota((HR, 128), 1))
    value = row_r + 1
    at_z = dz_r == iota((NZ, HR), 0)
    high = jnp.where(at_z, value >> 6, 0).astype(F32).astype(BF16)
    low = jnp.where(at_z, value & 63, 0).astype(F32).astype(BF16)
    wanted = (dot(high, column) * 64.0 + dot(low, column)).astype(I32) - 1
    for dz in range(NZ):
        s1[dz] = wanted[dz : dz + 1, :]
    k_c = dplane_c * NZ + dz_c
    k_r = dplane_r * NZ + dz_r
    pl.semaphore_wait(barrier, NZ - 1 + NPLANE - 1 + 1)

    for dz in (4, 3, 5, 2, 6, 1, 7):
        send(s1.at[dz], r1.at[dz], ssem.at[0], rsem.at[0], (plane * NZ + z_up[dz], mp))
    r1[0] = s1[0]
    wait_bytes(r1.at[pl.ds(0, NZ - 1)], rsem.at[0])
    sub = iota((8, 128), 0)
    gathered = jnp.zeros((8, 128), I32)
    for dz in range(NZ):
        gathered = jnp.where(sub == dz, r1[dz], gathered)
    s2[...] = gathered
    for dp in range(1, NPLANE):
        send(s2, r2.at[dp], ssem.at[1], rsem.at[1], (peer(plane, z, dp, 0), mp))
    r2[0] = gathered
    wait_bytes(r2.at[pl.ds(0, NPLANE - 1)], rsem.at[1])

    for load in loads[2:8]:
        load.start()
    table = r2[...].reshape(NG, 128)
    table_t = table.T
    lanes, subs = iota((NG, 128), 1), iota((NG, 128), 0)
    asked = []
    for j in range(CAP):
        asked.append(
            jnp.sum(jnp.where(lanes == (subs >> 3) * CAP + j, table, 0), axis=1, keepdims=True)
        )
        asked_ref[j : j + 1, :] = jnp.sum(
            jnp.where(subs == (lanes >> 3) * CAP + j, table_t, 0), axis=0, keepdims=True
        )

    loads[0].wait()
    loads[1].wait()
    for part in range(2):
        ks = slice(part * HALF, (part + 1) * HALF)
        pick = jnp.concatenate(
            [onehot(asked[j][ks] == iota((HALF, ROWS), 1)) for j in range(CAP)], 0
        )
        part_k = dot(pick, kbuf[...])
        part_v = dot(pick, vbuf[...])
        for j in range(CAP):
            rows = slice(j * HALF, (j + 1) * HALF)
            first = part * HALF * 16 + 4 * j
            for c in range(2):
                cols = slice(c * 128, (c + 1) * 128)
                fst[pl.ds(first + c, HALF, stride=16), :] = part_k[rows, cols]
                fst[pl.ds(first + 2 + c, HALF, stride=16), :] = part_v[rows, cols]
        kv_send[ks] = (
            fst[part * HALF * 16 : (part + 1) * HALF * 16, :].reshape(HALF, 16, 128).astype(BF16)
        )

        @pl.loop(part * NPLANE // 2, (part + 1) * NPLANE // 2)
        def _(dp):
            base = lax.rem(plane - dp + NPLANE, NPLANE) * NZ
            for dz in (4, 3, 5, 2, 6, 1, 7):
                k = dp * NZ + dz
                send(kv_send.at[k], kv_recv.at[k], ssem.at[2], rsem.at[2], (base + z_down[dz], mp))

    @pl.loop(1, NPLANE)
    def _(dp):
        base = lax.rem(plane - dp + NPLANE, NPLANE) * NZ
        send(kv_send.at[dp * NZ], kv_recv.at[dp * NZ], ssem.at[2], rsem.at[2], (base + z, mp))

    kv_recv[0] = kv_send[0]

    for load in loads[2:8]:
        load.wait()

    @pl.loop(0, ROWS // (2 * BLK))
    def _(step):
        both = pl.ds(pl.multiple_of(step * 2 * BLK, 2 * BLK), 2 * BLK)
        qm = head_stack(qbuf[both, :] * 0.125)
        gm = head_stack(gbuf[both, :])
        qms[step] = qm
        gms[step] = gm
        kts[step] = (kbuf[both, :] * 0.125).T
        ntr[step] = nbuf[both, :].T
        for half in range(2):
            rows = pl.ds(pl.multiple_of(step * 2 * BLK + half * BLK, BLK), BLK)
            s_own = dot(kbuf[rows, :], block_rows(qm, half), NT)
            d_own = dot(vbuf[rows, :], block_rows(gm, half), NT)
            top = jnp.max(s_own, 0, keepdims=True)
            p_own = jnp.exp2((s_own - top) * LOG2E)
            total = jnp.sum(p_own, 0, keepdims=True)
            term = jnp.sum(p_own * d_own, 0, keepdims=True)
            for h in range(HEADS_LOCAL):
                src = slice(h * BLK, (h + 1) * BLK)
                dst = slice((2 * h + half) * BLK, (2 * h + half + 1) * BLK)
                pbuf[step, :, dst] = p_own[:, src]
                dbuf[step, :, dst] = d_own[:, src]
                stats[step, 0:1, dst] = top[:, src]
                stats[step, 1:2, dst] = total[:, src]
                stats[step, 2:3, dst] = term[:, src]

    for j in range(CAP):
        pick = onehot(asked[j] == iota((NG, ROWS), 1))
        part_n = dot(pick, nbuf[...])
        for c in range(4):
            fst[pl.ds(4 * j + c, NG, stride=16), :] = part_n[:, c * 128 : (c + 1) * 128]
    n_send[...] = fst[...].reshape(NG, 16, 128).astype(BF16)
    far_acc[...] = jnp.zeros_like(far_acc)
    odd[...] = jnp.zeros_like(odd)

    @pl.loop(0, ROWS // 256)
    def _(i):
        base = pl.multiple_of(i * 256, 256)
        row = iota((256, NG), 0) + base
        for j in range(CAP):
            scat[pl.ds(base, 256), j * NG : (j + 1) * NG] = onehot(row == asked_ref[j : j + 1, :])


    wait_bytes(kv_recv.at[pl.ds(0, NG - 1)], rsem.at[2])
    fst[...] = kv_recv[...].astype(F32).reshape(NG * 16, 128)
    for j in range(CAP):
        for c in range(4):
            stack[j * NG : (j + 1) * NG, c * 128 : (c + 1) * 128] = fst[
                pl.ds(4 * j + c, NG, stride=16), :
            ].astype(BF16)
    place_mat = onehot(rank_c * NG + k_c == iota((HR, CAP * NG), 1))
    far_kv[...] = dot(place_mat, stack[...]).astype(BF16)
    far_kt[...] = (far_kv[:, 0:W] * 0.125).T

    mine_rows = pl.ds(pl.multiple_of(mp * W, W), W)
    other_rows = pl.ds(pl.multiple_of((1 - mp) * W, W), W)

    def scores(step, h):
        rows = slice(2 * h * BLK, 2 * (h + 1) * BLK)
        first = h // 2 * 128
        pair = slice(first, first + 128)
        return (
            dot(far_kv[:, pair], qms[step, rows, pair], NT),
            dot(far_kv[:, W + first : W + first + 128], gms[step, rows, pair], NT),
        )

    def soften(step, h, bias, s_far, d_far, buf):
        lanes = slice(2 * h * BLK, 2 * (h + 1) * BLK)
        top_own = stats[step, 0:1, lanes]
        top = jnp.maximum(
            top_own,
            jnp.maximum(
                jnp.max(s_far[0:BLK], 0, keepdims=True) - bias[0],
                jnp.max(s_far[BLK:], 0, keepdims=True) - bias[1],
            ),
        )
        p_far = jnp.concatenate(
            [
                jnp.exp2((s_far[0:BLK] - (top + bias[0])) * LOG2E),
                jnp.exp2((s_far[BLK:] - (top + bias[1])) * LOG2E),
            ],
            0,
        )
        share = jnp.exp2((top_own - top) * LOG2E)
        inv = 1.0 / (stats[step, 1:2, lanes] * share + jnp.sum(p_far, 0, keepdims=True))
        term = (stats[step, 2:3, lanes] * share + jnp.sum(p_far * d_far, 0, keepdims=True)) * inv
        prob_own = pbuf[step, :, lanes] * (share * inv)
        prob_far = p_far * inv
        buf[0, 0:BLK, lanes] = (prob_own * (dbuf[step, :, lanes] - term)).astype(BF16)
        buf[0, BLK:, lanes] = (prob_far * (d_far - term)).astype(BF16)
        buf[1, 0:BLK, lanes] = prob_own.astype(BF16)
        buf[1, BLK:, lanes] = prob_far.astype(BF16)

    def apply(step, buf, part):
        first = pl.multiple_of(step * 2 * BLK, 2 * BLK)
        if part < 2:
            stacked = (qms, gms)[part]
            for pair in range(2):
                span = slice(pair * 4 * BLK, (pair + 1) * 4 * BLK)
                lane = part * W + pair * 128
                far_acc[:, lane : lane + 128] += dot(
                    buf[part, BLK:, span], stacked[step, span, pair * 128 : (pair + 1) * 128]
                )
        elif part == 2:
            pieces = []
            for h in range(HEADS_LOCAL):
                heads = slice(h * E, (h + 1) * E)
                own_part = [
                    dot(
                        kts[step, heads, half * BLK : (half + 1) * BLK],
                        buf[0, 0:BLK, (2 * h + half) * BLK : (2 * h + half + 1) * BLK],
                    )
                    for half in range(2)
                ]
                pieces.append(
                    dot(far_kt[heads, :], buf[0, BLK:, 2 * h * BLK : 2 * (h + 1) * BLK])
                    + jnp.concatenate(own_part, 1)
                )
            grads[pl.ds(first, 2 * BLK), 0:W] = jnp.concatenate(pieces, 0).T.astype(BF16)
        else:
            for i, stacked in enumerate((qms, gms)):
                for half in range(2):
                    rows = pl.ds(pl.multiple_of(first + half * BLK, BLK), BLK)
                    grads[rows, (i + 1) * W : (i + 2) * W] = dot(
                        block_lanes(buf[i, 0:BLK, :], half), block_rows(stacked[step], half)
                    ).astype(BF16)

    def attend(step, buf, before, buf_before):
        second = ((iota((1, 2 * BLK), 1) >> 7) & 1) == 1
        bias = []
        for h in range(2):
            each = [
                jnp.where(pattern_ref[h, 2 * step + half] > 0, 0.0, 1e30).astype(F32)
                for half in range(2)
            ]
            bias.append(jnp.where(second, each[1], each[0]))
        ready = scores(step, 0)
        for h in range(HEADS_LOCAL):
            now = ready
            if h + 1 < HEADS_LOCAL:
                ready = scores(step, h + 1)
            apply(before, buf_before, h)
            soften(step, h, bias, now[0], now[1], buf)

    def attend_pair(t):
        attend(2 * t, even, jnp.maximum(2 * t - 1, 0), odd)
        attend(2 * t + 1, odd, 2 * t, even)

    def project(step):
        both = pl.ds(pl.multiple_of(step * 2 * BLK, 2 * BLK), 2 * BLK)
        kept = jnp.zeros((2 * BLK, W), F32)
        given = jnp.zeros((2 * BLK, W), F32)
        for i in range(3):
            grad = grads[both, i * W : (i + 1) * W]
            kept += dot(grad, wbuf[i, mine_rows, :], NT)
            given += dot(grad, wbuf[i, other_rows, :], NT)
        mine[both, :] = kept
        gbuf[both, :] = given.astype(BF16)
        send(gbuf.at[both], e_recv.at[both], ssem.at[6], rsem.at[6], twin)

    first_plane = mp * (NPLANE // 2)

    @pl.loop(0, NPLANE // 2)
    def _(i):
        dp = first_plane + i
        base = lax.rem(plane - dp + NPLANE, NPLANE) * NZ
        for dz in range(1, NZ):
            send(
                n_send.at[dp * NZ + dz], n_recv.at[i * NZ + dz], ssem.at[3], rsem.at[3],
                (base + z_down[dz], mp),
            )

    @pl.loop(1, NPLANE // 2)
    def _(i):
        dp = first_plane + i
        base = lax.rem(plane - dp + NPLANE, NPLANE) * NZ
        send(n_send.at[dp * NZ], n_recv.at[i * NZ], ssem.at[3], rsem.at[3], (base + z, mp))

    @pl.when(mp == 1)
    def _():
        base = lax.rem(plane + NPLANE // 2, NPLANE) * NZ
        send(n_send.at[HALF], n_recv.at[0], ssem.at[4], rsem.at[4], (base + z, mp))

    @pl.when(mp == 0)
    def _():
        n_recv[0] = n_send[0]

    steps = ROWS // (2 * BLK)
    early = steps - 2

    @pl.loop(0, early // 2)
    def _(t):
        attend_pair(t)

    k_ch = k_c - mp * HALF
    slot_c = jnp.where((k_ch >= 0) & (k_ch < HALF), rank_c * HALF + k_ch, -1)
    k_rh = k_r - mp * HALF
    slot_r = jnp.where((k_rh >= 0) & (k_rh < HALF), rank_r * HALF + k_rh, -1)
    wait_bytes(n_recv.at[pl.ds(0, HALF - 1)], rsem.at[3])

    @pl.when(mp == 1)
    def _():
        wait_bytes(n_recv.at[0], rsem.at[4])

    fst[0 : HALF * 16, :] = n_recv[...].astype(F32).reshape(HALF * 16, 128)
    for j in range(CAP):
        for c in range(4):
            stack[j * HALF : (j + 1) * HALF, c * 128 : (c + 1) * 128] = fst[
                pl.ds(4 * j + c, HALF, stride=16), :
            ].astype(BF16)
    place_half = onehot(slot_c == iota((HR, CAP * HALF), 1))
    fn_send[...] = dot(place_half, stack[0 : CAP * HALF, :]).astype(BF16)
    send(fn_send, fn_recv, ssem.at[5], rsem.at[5], twin)

    @pl.loop(early // 2, steps // 2)
    def _(t):
        attend_pair(t)

    for part in range(4):
        apply(steps - 1, odd, part)

    dk_far = far_acc[:, 0:W].astype(BF16)
    dv_far = far_acc[:, W : 2 * W].astype(BF16)
    far_kv[...] = (dot(dk_far, wbuf[1], NT) + dot(dv_far, wbuf[2], NT)).astype(BF16)
    send(far_kv, t_recv, ssem.at[7], rsem.at[7], twin)
    wait_bytes(fn_recv, rsem.at[5])
    far_nodes = fn_send[...] + fn_recv[...]

    edge = 3 * W // 2
    for i in range(3):
        columns = slice(i * W, (i + 1) * W)
        part = jnp.zeros((2 * W, W), F32)
        for step in range(steps):
            part += dot(ntr[step], grads[step * 2 * BLK : (step + 1) * 2 * BLK, columns])
        if i == 1:
            part += dot(far_nodes, dk_far, TN)
        if i == 2:
            part += dot(far_nodes, dv_far, TN)
        gw[:, columns] = part
    a_send[...] = gw[:, 0:edge].astype(BF16).reshape(NY, 128, edge)
    for d in range(1, NY):
        yy = lax.rem(y + d, NY)
        send(a_send.at[yy], a_recv.at[d - 1], ssem.at[8], rsem.at[8], ((yy * NX + x) * NZ + z, mp))
    for yy in range(NY):
        for xx in range(NX):
            first = yy * 128 + xx * 32
            b_send[xx, yy] = gw[first : first + 32, edge:].astype(BF16)
    for d in range(1, NX):
        xx = lax.rem(x + d, NX)
        send(b_send.at[xx], b_recv.at[d - 1], ssem.at[14], rsem.at[14], ((y * NX + xx) * NZ + z, mp))

    place_t = onehot(slot_r == iota((CAP * HALF, HR), 0))
    wait_bytes(t_recv, rsem.at[7])
    summed = (far_kv[...].astype(F32) + t_recv[...].astype(F32)).astype(BF16)
    placed = dot(place_t, summed)
    for j in range(CAP):
        for c in range(4):
            fst[pl.ds(4 * j + c, HALF, stride=16), :] = placed[
                j * HALF : (j + 1) * HALF, c * 128 : (c + 1) * 128
            ]
    z_send[...] = fst[0 : HALF * 16, :].reshape(HALF, 16, 128).astype(BF16)

    @pl.loop(0, NPLANE // 2)
    def _(i):
        base = lax.rem(plane + first_plane + i, NPLANE) * NZ
        for dz in (4, 3, 5, 2, 6, 1, 7):
            k = i * NZ + dz
            send(z_send.at[k], z_recv.at[k], ssem.at[9], rsem.at[9], (base + z_up[dz], mp))

    @pl.loop(1, NPLANE // 2)
    def _(i):
        base = lax.rem(plane + first_plane + i, NPLANE) * NZ
        send(z_send.at[i * NZ], z_recv.at[i * NZ], ssem.at[9], rsem.at[9], (base + z, mp))

    @pl.when(mp == 1)
    def _():
        base = lax.rem(plane + NPLANE // 2, NPLANE) * NZ
        send(z_send.at[0], z_recv.at[0], ssem.at[10], rsem.at[10], (base + z, mp))

    @pl.when(mp == 0)
    def _():
        z_recv[0] = z_send[0]

    @pl.loop(0, 4)
    def _(step):
        project(step)

    @pl.loop(4, steps)
    def _(step):
        project(step)

    wait_bytes(a_recv, rsem.at[8])
    own = gw[pl.ds(pl.multiple_of(y * 128, 128), 128), 0:edge]
    for d in range(NY - 1):
        own += a_recv[d].astype(F32)
    a_sum[...] = own
    a2_send[...] = own.astype(BF16).reshape(NX, 32, edge)
    for d in range(1, NX):
        xx = lax.rem(x + d, NX)
        send(a2_send.at[xx], a2_recv.at[d - 1], ssem.at[11], rsem.at[11], ((y * NX + xx) * NZ + z, mp))
    wait_bytes(b_recv, rsem.at[14])
    for yy in range(NY):
        own = gw[pl.ds(pl.multiple_of(yy * 128 + x * 32, 32), 32), edge:]
        for d in range(NX - 1):
            own += b_recv[d, yy].astype(F32)
        b_sum[yy * 32 : (yy + 1) * 32, :] = own
        b2_send[yy] = own.astype(BF16)
    for d in range(1, NY):
        yy = lax.rem(y + d, NY)
        send(b2_send.at[yy], b2_recv.at[d - 1], ssem.at[15], rsem.at[15], ((yy * NX + x) * NZ + z, mp))

    wait_bytes(a2_recv, rsem.at[11])
    wait_bytes(b2_recv, rsem.at[15])
    own_a = a_sum[pl.ds(pl.multiple_of(x * 32, 32), 32), :]
    own_b = b_sum[pl.ds(pl.multiple_of(y * 32, 32), 32), :]
    for d in range(NX - 1):
        own_a += a2_recv[d].astype(F32)
        own_b += b2_recv[d].astype(F32)
    for zz in range(NZ):
        for c in range(3):
            zz_send[zz, 4 * c : 4 * c + 4, :] = own_a[4 * zz : 4 * zz + 4, c * 128 : (c + 1) * 128]
            zz_send[zz, 4 * c + 12 : 4 * c + 16, :] = own_b[
                4 * zz : 4 * zz + 4, c * 128 : (c + 1) * 128
            ]
    for d in (4, 3, 5, 2, 6, 1, 7):
        send(
            zz_send.at[z_up[d]], zz_recv.at[d], ssem.at[12], rsem.at[12], (plane * NZ + z_up[d], mp)
        )
    zz_recv[0] = zz_send[z]

    wait_bytes(z_recv.at[pl.ds(0, HALF - 1)], rsem.at[9])

    @pl.when(mp == 1)
    def _():
        wait_bytes(z_recv.at[0], rsem.at[10])

    fst[0 : HALF * 16, :] = z_recv[...].astype(F32).reshape(HALF * 16, 128)
    for j in range(CAP):
        for c in range(2):
            x_send[j, :, c * 128 : (c + 1) * 128] = fst[
                pl.ds(4 * j + 2 * (1 - mp) + c, HALF, stride=16), :
            ].astype(BF16)
    send(x_send, z_full.at[:, mp], ssem.at[13], rsem.at[13], twin)
    for j in range(CAP):
        for c in range(2):
            z_full[j, mp, :, c * 128 : (c + 1) * 128] = fst[
                pl.ds(4 * j + 2 * mp + c, HALF, stride=16), :
            ].astype(BF16)
    wait_bytes(e_recv, rsem.at[6])
    mine[...] += e_recv[...].astype(F32)

    wait_bytes(x_send, rsem.at[13])
    far = z_full[...].reshape(CAP * NG, W)

    @pl.loop(0, ROWS // 512)
    def _(i):
        rows = pl.ds(pl.multiple_of(i * 512, 512), 512)
        nodes_out[rows, :] = (mine[rows, :] + dot(scat[rows, :], far)).astype(BF16)

    wait_bytes(zz_recv.at[pl.ds(0, NZ - 1)], rsem.at[12])
    final = zz_recv[0]
    for d in range(1, NZ):
        final += zz_recv[d]
    for c in range(6):
        weights_out[c // 2, :, (c % 2) * 128 : (c % 2 + 1) * 128] = final[4 * c : 4 * c + 4, :]

    wait_bytes(s1.at[pl.ds(0, NZ - 1)], ssem.at[0])
    wait_bytes(r2.at[pl.ds(0, NPLANE - 1)], ssem.at[1])
    wait_bytes(kv_send.at[pl.ds(0, NG - 1)], ssem.at[2])
    wait_bytes(n_recv.at[pl.ds(0, HALF - 1)], ssem.at[3])
    wait_bytes(fn_recv, ssem.at[5])
    wait_bytes(e_recv, ssem.at[6])
    wait_bytes(t_recv, ssem.at[7])
    wait_bytes(a_recv, ssem.at[8])
    wait_bytes(b_recv, ssem.at[14])
    wait_bytes(z_recv.at[pl.ds(0, HALF - 1)], ssem.at[9])
    wait_bytes(a2_recv, ssem.at[11])
    wait_bytes(b2_recv, ssem.at[15])
    wait_bytes(zz_recv.at[pl.ds(0, NZ - 1)], ssem.at[12])
    wait_bytes(x_send, ssem.at[13])

    @pl.when(mp == 1)
    def _():
        wait_bytes(n_recv.at[0], ssem.at[4])
        wait_bytes(z_recv.at[0], ssem.at[10])


VM = pl.BlockSpec(memory_space=pltpu.VMEM)
HBM = pl.BlockSpec(memory_space=pltpu.HBM)
LIMIT = 56 * 1024 * 1024


def on_device(
    nodes_in, query, keys, values, grad_attn, w_query, w_key, w_value, halo_owner, halo_row, pattern
):
    dma = pltpu.SemaphoreType.DMA
    vm = pltpu.VMEM
    grad_nodes, grad_weights = pl.pallas_call(
        layer_kernel,
        out_shape=(
            jax.ShapeDtypeStruct((ROWS, W), BF16),
            jax.ShapeDtypeStruct((3, 4, W), F32),
        ),
        in_specs=[HBM] * 11,
        out_specs=(VM, VM),
        scratch_shapes=[
            vm((ROWS, W), BF16),
            vm((ROWS, W), BF16),
            vm((ROWS, W), BF16),
            vm((ROWS, W), BF16),
            vm((ROWS, 2 * W), BF16),
            vm((3, 2 * W, W), BF16),
            vm((NZ, 1, 128), I32),
            vm((NZ, 1, 128), I32),
            vm((8, 128), I32),
            vm((NPLANE, 8, 128), I32),
            vm((NG * 16, 128), F32),
            vm((NG, 16, 128), BF16),
            vm((NG, 16, 128), BF16),
            vm((NG, 16, 128), BF16),
            vm((HALF, 16, 128), BF16),
            vm((CAP * NG, 2 * W), BF16),
            vm((HR, 2 * W), BF16),
            vm((HR, 2 * W), BF16),
            pltpu.SMEM((2, ROWS // BLK), I32),
            vm((1, HR), I32),
            vm((1, HR), I32),
            vm((8, 128), I32),
            vm((HR, 2 * W), BF16),
            vm((W, HR), BF16),
            vm((HR, 2 * W), F32),
            vm((ROWS // 256, BLK, 8 * BLK), F32),
            vm((ROWS // 256, BLK, 8 * BLK), F32),
            vm((ROWS // 256, 8, 8 * BLK), F32),
            vm((2 * W, 3 * W), F32),
            vm((ROWS, W), F32),
            vm((ROWS, W), BF16),
            vm((ROWS // 256, 8 * BLK, W), BF16),
            vm((ROWS // 256, 8 * BLK, W), BF16),
            vm((ROWS // 256, W, 2 * BLK), BF16),
            vm((ROWS // 256, 2 * W, 2 * BLK), BF16),
            vm((ROWS, CAP * NG), BF16),
            vm((ROWS, 3 * W), BF16),
            vm((2, 3 * BLK, 8 * BLK), BF16),
            vm((2, 3 * BLK, 8 * BLK), BF16),
            vm((HR, 2 * W), BF16),
            vm((HALF, 16, 128), BF16),
            vm((HALF, 16, 128), BF16),
            vm((CAP, HALF, W), BF16),
            vm((CAP, 2, HALF, W), BF16),
            vm((NY, 128, 3 * W // 2), BF16),
            vm((NY - 1, 128, 3 * W // 2), BF16),
            vm((NX, NY, 32, 3 * W // 2), BF16),
            vm((NX - 1, NY, 32, 3 * W // 2), BF16),
            vm((128, 3 * W // 2), F32),
            vm((128, 3 * W // 2), F32),
            vm((NX, 32, 3 * W // 2), BF16),
            vm((NX - 1, 32, 3 * W // 2), BF16),
            vm((NY, 32, 3 * W // 2), BF16),
            vm((NY - 1, 32, 3 * W // 2), BF16),
            vm((NZ, 24, 128), F32),
            vm((NZ, 24, 128), F32),
            dma((11,)),
            dma((16,)),
            dma((20,)),
        ],
        compiler_params=pltpu.CompilerParams(
            collective_id=0, has_side_effects=True, vmem_limit_bytes=LIMIT
        ),
        name="layer",
    )(
        pattern.T, halo_owner.reshape(1, HR), halo_row.reshape(1, HR),
        query, keys, values, grad_attn, nodes_in, w_query, w_key, w_value,
    )
    return grad_nodes, jnp.transpose(grad_weights, (1, 0, 2))


def solution(mesh):
    in_specs = (
        P("graph", None),
        P("graph", "mp"),
        P("graph", "mp"),
        P("graph", "mp"),
        P("graph", "mp"),
        P(None, "mp"),
        P(None, "mp"),
        P(None, "mp"),
        P("graph", None),
        P("graph"),
        P("graph", None),
    )
    out_specs = (P("graph", "mp"), P("graph", None, "mp"))
    return jax.shard_map(
        on_device, mesh=mesh, in_specs=in_specs, out_specs=out_specs, check_vma=False
    )
```
